256 devices in a mesh: gx: 8 (over z), gy: 32 (over y, x, core).
Axes of the slice: x: 4, y: 4, z: 8, core: 2. Of those that a mesh axis runs over, the one named last changes fastest.
Arguments:
- populations: float32 [2, 7, 128, 256, 512], P(None, None, 'gx', 'gy'), may hold values from 0.02 to 0.3
- conductivity: float32 [128, 256, 512], P('gx', 'gy'), may hold values from 0.5 to 4
- deposit_mask: int32 [128, 256, 512], P('gx', 'gy'), may hold values 0 or 1
- electrode_flags: int32 [128, 256, 512], P('gx', 'gy'), may hold values 0 or 1
- previous_potential: float32 [128, 256, 512], P('gx', 'gy'), may hold values from -9 to 9
Outputs:
- potential: float32 [128, 256, 512], P('gx', 'gy')
- populations_next: float32 [2, 7, 128, 256, 512], P(None, None, 'gx', 'gy')
The draws below stay inside these ranges and needn't reach their ends.
All inputs are finite; a program needn't handle non-finite values. No bound on the sum of `deposit_mask` or of `electrode_flags` on one device may be relied on, other than what follows from the above.
Results may differ from the reference program's by a relative error of at most 0.0003.
Values sent between devices are 32-bit elements; how exact they have to be, the bound alone decides.
No kernel may reach another device: no remote copies, remote signals or barrier semaphores. Data moves between devices by JAX's collectives and lax.ppermute only.
A program may use at most 128 MiB of HBM per device.

```python
import math
import jax
import jax.numpy as jnp

NZ = 512
ITERS = 3
NX = 128
NY = 256


def draw_previous_potential(key, part):
    across = jnp.arange(NX, dtype=jnp.float32) / max(NX - 1, 1)
    rising = (1.0 + 2.0 * across)[:, None, None]
    noise_base = jnp.clip(jax.random.normal(key, (NX, NY, NZ), jnp.float32), -6.0, 6.0)
    return 0.5 * noise_base * rising


def set_ends(result, key, smallest, top_value):
    shape = result.shape
    index_at = [jax.random.randint(jax.random.fold_in(key, axis), (), 0, shape[axis]) for axis in range(len(shape))]
    result = result.at[tuple(index_at)].set(smallest)
    longest = shape.index(max(shape))
    index_at[longest] = (index_at[longest] + 1) % shape[longest]
    return result.at[tuple(index_at)].set(top_value)


def shard_levels(stream_key, extent, shards, smallest, top_value):
    level, own = 1.0, jax.random.fold_in(stream_key, 6)
    for axis_at, blocks in shards:
        draws = jnp.exp(jax.random.uniform(jax.random.fold_in(own, axis_at), (blocks,), jnp.float32, smallest / len(shards), top_value / len(shards)))
        level = level * jnp.repeat(draws, extent[axis_at] // blocks).reshape([-1 if axis == axis_at else 1 for axis in range(len(extent))])
    return level


def setup_inputs(seed: int = 0) -> dict:
    key_of = jax.random.split(jax.random.key(seed), 6)
    populations = jnp.clip(0.02 + 0.28 * jax.random.uniform(key_of[0], (2, 7, NX, NY, NZ), jnp.float32) ** shard_levels(key_of[0], (2, 7, NX, NY, NZ), ((2, 8), (3, 32)), -0.2, 0.2), 0.02, 0.3)
    conductivity = jnp.clip(jnp.exp(math.log(4.0) - 2.0794415 * jax.random.uniform(key_of[1], (NX, NY, NZ), jnp.float32) ** shard_levels(key_of[1], (NX, NY, NZ), ((0, 8), (1, 32)), -0.2, 0.2)), 0.5, 4.0)
    deposit_mask = set_ends((jax.random.randint(key_of[2], (NX, NY, NZ), 0, 8) < 1).astype(jnp.int32), jax.random.fold_in(key_of[2], 1), 0, 1)
    electrode_flags = set_ends((jax.random.randint(key_of[3], (NX, NY, NZ), 0, 16) < 1).astype(jnp.int32), jax.random.fold_in(key_of[3], 1), 0, 1)
    previous_potential = draw_previous_potential(jax.random.fold_in(key_of[5], 71), 0)
    return dict(populations=populations, conductivity=conductivity, deposit_mask=deposit_mask, electrode_flags=electrode_flags, previous_potential=previous_potential)


SCREEN_RATE = 0.01
WEIGHTS = (0.25, 0.125, 0.125, 0.125, 0.125, 0.125, 0.125)
OPPOSITE = (0, 2, 1, 4, 3, 6, 5)
DRIFT_COEF = (-0.02, 0.016)
RELAX_TIME = (0.8, 1.1)


def harmonic(left_cell, right_cell):
    return 2.0 * left_cell * right_cell / (left_cell + right_cell)


def harmonic_faces(sigma_pad):
    middle = sigma_pad[1:-1, 1:-1]
    upper_z = jnp.concatenate([middle[:, :, 1:], middle[:, :, -1:]], axis=2)
    lower_z = jnp.concatenate([middle[:, :, :1], middle[:, :, :-1]], axis=2)
    return (harmonic(middle, sigma_pad[2:, 1:-1]), harmonic(middle, sigma_pad[:-2, 1:-1]),
            harmonic(middle, sigma_pad[1:-1, 2:]), harmonic(middle, sigma_pad[1:-1, :-2]),
            harmonic(middle, upper_z), harmonic(middle, lower_z))


def laplace(padded, weights):
    middle = padded[1:-1, 1:-1]
    zero_layer = jnp.zeros_like(middle[:, :, :1])
    above_z = jnp.concatenate([middle[:, :, 1:], zero_layer], axis=2)
    below_z = jnp.concatenate([zero_layer, middle[:, :, :-1]], axis=2)
    summed = weights[0] * (middle - padded[2:, 1:-1]) + weights[1] * (middle - padded[:-2, 1:-1])
    summed = summed + weights[2] * (middle - padded[1:-1, 2:]) + weights[3] * (middle - padded[1:-1, :-2])
    summed = summed + weights[4] * (middle - above_z) + weights[5] * (middle - below_z)
    return summed + SCREEN_RATE * middle


def collide(populations_in, potential_pad):
    middle = potential_pad[1:-1, 1:-1]
    zero_layer = jnp.zeros_like(middle[:, :, :1])
    grad_x = 0.5 * (potential_pad[2:, 1:-1] - potential_pad[:-2, 1:-1])
    grad_y = 0.5 * (potential_pad[1:-1, 2:] - potential_pad[1:-1, :-2])
    grad_z = 0.5 * (jnp.concatenate([middle[:, :, 1:], zero_layer], axis=2)
                    - jnp.concatenate([zero_layer, middle[:, :, :-1]], axis=2))
    density = jnp.sum(populations_in, axis=1)
    collided = []
    for species in range(2):
        velo_x = DRIFT_COEF[species] * grad_x
        velo_y = DRIFT_COEF[species] * grad_y
        velo_z = DRIFT_COEF[species] * grad_z
        projected = (None, velo_x, -velo_x, velo_y, -velo_y, velo_z, -velo_z)
        relax_rate = 1.0 / RELAX_TIME[species]
        out_rows = []
        for lattice_dir in range(7):
            if lattice_dir == 0:
                balance = WEIGHTS[0] * density[species]
            else:
                balance = WEIGHTS[lattice_dir] * density[species] * (1.0 + 4.0 * projected[lattice_dir])
            current = populations_in[species, lattice_dir]
            out_rows.append(current - relax_rate * (current - balance))
        collided.append(jnp.stack(out_rows, axis=0))
    return jnp.stack(collided, axis=0)


def stream(collided_pad, solid_pad):
    middle = collided_pad[:, :, 1:-1, 1:-1]
    solid_mid = solid_pad[1:-1, 1:-1]
    zero_layer = jnp.zeros_like(middle[:, 0, :, :, :1])
    one_layer = jnp.ones_like(solid_mid[:, :, :1])
    sources = (
        (collided_pad[:, 1, :-2, 1:-1], solid_pad[:-2, 1:-1]),
        (collided_pad[:, 2, 2:, 1:-1], solid_pad[2:, 1:-1]),
        (collided_pad[:, 3, 1:-1, :-2], solid_pad[1:-1, :-2]),
        (collided_pad[:, 4, 1:-1, 2:], solid_pad[1:-1, 2:]),
        (jnp.concatenate([zero_layer, middle[:, 5, :, :, :-1]], axis=3),
         jnp.concatenate([one_layer, solid_mid[:, :, :-1]], axis=2)),
        (jnp.concatenate([middle[:, 6, :, :, 1:], zero_layer], axis=3),
         jnp.concatenate([solid_mid[:, :, 1:], one_layer], axis=2)),
    )
    arrived = [middle[:, 0]]
    for lattice_dir in range(1, 7):
        source, blocked = sources[lattice_dir - 1]
        arrived.append(jnp.where(blocked > 0.5, middle[:, OPPOSITE[lattice_dir]], source))
    return jnp.stack(arrived, axis=1) * (1.0 - solid_mid)


def wrap_field(values):
    return jnp.pad(values, ((1, 1), (1, 1), (0, 0)), mode="wrap")


def wrap_pops(values):
    return jnp.pad(values, ((0, 0), (0, 0), (1, 1), (1, 1), (0, 0)), mode="wrap")


def reference(populations, conductivity, deposit_mask, electrode_flags, previous_potential):
    solid_cell = deposit_mask.astype(jnp.float32)
    sigma_cell = conductivity * (1.0 + 3.0 * solid_cell)
    pinned = electrode_flags.astype(jnp.float32)
    unknown = 1.0 - pinned
    weights = harmonic_faces(wrap_field(sigma_cell))
    solid_pad = wrap_field(solid_cell)

    def apply_op(values):
        return unknown * laplace(wrap_field(unknown * values), weights) + pinned * values

    density = jnp.sum(populations, axis=1)
    charge = 2.0 * density[0] - 2.0 * density[1]
    residual = unknown * (charge - laplace(wrap_field(previous_potential), weights))
    direction = residual
    correction = jnp.zeros_like(residual)
    norm_now = jnp.sum(residual * residual)
    for sweep in range(ITERS):
        mapped = apply_op(direction)
        step_size = norm_now / jnp.sum(direction * mapped)
        correction = correction + step_size * direction
        residual = residual - step_size * mapped
        if sweep + 1 < ITERS:
            norm_next = jnp.sum(residual * residual)
            direction = residual + (norm_next / norm_now) * direction
            norm_now = norm_next
    potential = previous_potential + correction
    collided = collide(populations, wrap_field(potential))
    return potential, stream(wrap_pops(collided), solid_pad)
```

```python
import jax
import jax.numpy as jnp
from jax import lax
from jax.experimental import pallas as pl
from jax.experimental.pallas import tpu as pltpu
from jax.sharding import PartitionSpec as P

SCREEN_RATE = 0.01
WEIGHTS = (0.25, 0.125, 0.125, 0.125, 0.125, 0.125, 0.125)
OPPOSITE = (0, 2, 1, 4, 3, 6, 5)
DRIFT_COEF = (-0.02, 0.016)
RELAX_TIME = (0.8, 1.1)

H = 5
T = 8
SCALE = 0.0625

PREV, SIGMA, FLAGS, CHARGE = (0, 5), (5, 5), (10, 4), (14, 3)
DENS, POP, SOLID = 17, 19, 21
FACE_ROWS = 24

CORNER = (
    ("prev", 1, 4, 0, 0), ("prev", 2, 3, 0, 4), ("prev", 4, 1, 0, 7),
    ("sigma", 1, 4, 1, 0), ("sigma", 2, 3, 1, 4), ("sigma", 4, 1, 1, 7),
    ("prev", 3, 2, 2, 0), ("sigma", 3, 2, 2, 2), ("flags", 2, 2, 2, 4), ("charge", 2, 2, 2, 6),
    ("flags", 1, 3, 3, 0), ("charge", 1, 3, 3, 3), ("flags", 3, 1, 3, 6), ("charge", 3, 1, 3, 7),
)
SPAN = {"prev": PREV, "sigma": SIGMA, "flags": FLAGS, "charge": CHARGE}
VMEM = pl.BlockSpec(memory_space=pltpu.VMEM)
F32 = jnp.float32


def params(mib):
    return pltpu.CompilerParams(vmem_limit_bytes=mib * 1024 * 1024)


def pack_kernel(pops, cond, mask, flags, prev, charge, sigma, xlo, xhi, ylo, yhi):
    nx = cond.shape[0]

    def fields(x):
        d0 = pops[0, 0, x]
        d1 = pops[1, 0, x]
        for i in range(1, 7):
            d0 = d0 + pops[0, i, x]
            d1 = d1 + pops[1, i, x]
        solid = mask[x].astype(F32)
        return d0, d1, 2.0 * d0 - 2.0 * d1, cond[x] * (1.0 + 3.0 * solid), solid

    def row(x, _):
        d0, d1, ch, sg, solid = fields(x)
        charge[x] = ch
        sigma[x] = sg
        fl = flags[x].astype(F32)
        pv = prev[x]
        for out, up, way in ((ylo, False, 4), (yhi, True, 3)):
            def put(first, n, value, skip=0):
                at = T - n - skip if up else skip
                out[x, first:first + n] = value[at:at + n]
            put(*PREV, pv)
            put(*SIGMA, sg)
            put(*FLAGS, fl)
            put(*CHARGE, ch, 1)
            put(DENS, 1, d0)
            put(DENS + 1, 1, d1)
            put(POP, 1, pops[0, way, x])
            put(POP + 1, 1, pops[1, way, x])
            put(SOLID, 1, solid)
            put(SOLID + 1, 2, solid)
        return 0

    lax.fori_loop(0, nx, row, 0)
    for out, up, way in ((xlo, False, 2), (xhi, True, 1)):
        def start(n, skip=0):
            return nx - n - skip if up else skip
        n = PREV[1]
        out[PREV[0]:PREV[0] + n] = prev[start(n):start(n) + n]
        out[SIGMA[0]:SIGMA[0] + n] = sigma[start(n):start(n) + n]
        n = FLAGS[1]
        out[FLAGS[0]:FLAGS[0] + n] = flags[start(n):start(n) + n].astype(F32)
        n = CHARGE[1]
        out[CHARGE[0]:CHARGE[0] + n] = charge[start(n, 1):start(n, 1) + n]
        edge = start(1)
        d0, d1, _, _, solid = fields(edge)
        out[DENS] = d0
        out[DENS + 1] = d1
        out[POP] = pops[0, way, edge]
        out[POP + 1] = pops[1, way, edge]
        out[SOLID] = solid


def x_row(buf, side, name, distance):
    if name == "charge":
        if distance == 1:
            return 2.0 * buf[DENS] - 2.0 * buf[DENS + 1]
        return buf[CHARGE[0] + (4 - distance if side == 0 else distance - 2)]
    first, n = SPAN[name]
    return buf[first + (n - distance if side == 0 else distance - 1)]


def corner_kernel(xlo, xhi, clo, chi):
    for side, buf in ((0, xlo), (1, xhi)):
        for name, distance, n, tile, at in CORNER:
            value = x_row(buf, side, name, distance)
            clo[4 * side + tile, at:at + n] = value[:n]
            chi[4 * side + tile, at:at + n] = value[T - n:]


def harmonic(a, b):
    return 2.0 * a * b / (a + b)


def krylov_kernel(sigma, charge, flags, prev, xlo, xhi, ylo, yhi, clo, chi,
                  pv, v0, v1, v2, moments, sg, un, ch, wx, wy, wz):
    nx, _, nz = sigma.shape
    top = nx + H
    px = nx + 2 * H

    def own(x, _):
        at = x + H
        pv[at, T:2 * T] = prev[x]
        sg[at, T:2 * T] = sigma[x]
        un[at, T:2 * T] = 1.0 - flags[x].astype(F32)
        ch[at, T:2 * T] = charge[x]
        for buf, up in ((ylo, False), (yhi, True)):
            def put(ref, first, n, skip=0, one=False):
                to = 2 * T + skip if up else T - n - skip
                value = buf[x, first:first + n]
                ref[at, to:to + n] = 1.0 - value if one else value
            put(pv, *PREV)
            put(sg, *SIGMA)
            put(un, *FLAGS, 0, True)
            put(ch, *CHARGE, 1)
            to = 2 * T if up else T - 1
            ch[at, to:to + 1] = 2.0 * buf[x, DENS:DENS + 1] - 2.0 * buf[x, DENS + 1:DENS + 2]
        return 0

    lax.fori_loop(0, nx, own, 0)
    for side, buf in ((0, xlo), (1, xhi)):
        for distance in range(1, 6):
            at = H - distance if side == 0 else top - 1 + distance
            pv[at, T:2 * T] = x_row(buf, side, "prev", distance)
            sg[at, T:2 * T] = x_row(buf, side, "sigma", distance)
            if distance < 5:
                un[at, T:2 * T] = 1.0 - x_row(buf, side, "flags", distance)
                ch[at, T:2 * T] = x_row(buf, side, "charge", distance)
        for name, distance, n, tile, row in CORNER:
            at = H - distance if side == 0 else top - 1 + distance
            ref = {"prev": pv, "sigma": sg, "flags": un, "charge": ch}[name]
            for buf_y, to in ((clo, T - n), (chi, 2 * T)):
                value = buf_y[4 * side + tile, row:row + n]
                ref[at, to:to + n] = 1.0 - value if name == "flags" else value

    lane = lax.broadcasted_iota(jnp.int32, (3 * T, nz), 1)
    first, last = lane == 0, lane == nz - 1

    def faces(x, _):
        a = sg[x]
        wx[x] = harmonic(a, sg[jnp.minimum(x + 1, px - 1)])
        wy[x] = harmonic(a, pltpu.roll(a, 3 * T - 1, 0))
        wz[x] = harmonic(a, jnp.where(last, a, pltpu.roll(a, nz - 1, 1)))
        return 0

    lax.fori_loop(0, px, faces, 0)

    def flux_x(ref, x):
        return wx[x] * (ref[x] - ref[x + 1])

    def laplace(ref, x, below):
        m = ref[x]
        fx = wx[x] * (m - ref[x + 1])
        fy = wy[x] * (m - pltpu.roll(m, 3 * T - 1, 0))
        fz = wz[x] * (m - jnp.where(last, 0.0, pltpu.roll(m, nz - 1, 1)))
        s = fx - below
        s = s + (fy - pltpu.roll(fy, 1, 0))
        s = s + (fz + jnp.where(first, sg[x] * m, -pltpu.roll(fz, 1, 1)))
        return s + SCREEN_RATE * m, fx

    def sweep(src, lo, hi, store):
        def body(x, below):
            value, below = laplace(src, x, below)
            store(x, value)
            return below
        lax.fori_loop(lo, hi, body, flux_x(src, lo - 1))

    def store_v0(x, value):
        v0[x] = un[x] * (ch[x] - value)

    def apply_to(src, dst):
        def store(x, value):
            u = un[x]
            dst[x] = (u * value + (1.0 - u) * src[x]) * SCALE
        return store

    sweep(pv, H - 4, top + 4, store_v0)
    sweep(v0, H - 3, top + 3, apply_to(v0, v1))
    sweep(v1, H - 2, top + 2, apply_to(v1, v2))

    def last_sweep(x, carry):
        below, acc = carry
        value, below = laplace(v2, x, below)
        u = un[x, T:2 * T]
        a, b, c = v0[x, T:2 * T], v1[x, T:2 * T], v2[x, T:2 * T]
        d = (u * value[T:2 * T] + (1.0 - u) * c) * SCALE
        terms = (a * a, a * b, b * b, b * c, c * c, c * d)
        return below, tuple(s + t for s, t in zip(acc, terms))

    zero = jnp.zeros((T, nz), F32)
    _, acc = lax.fori_loop(H, top, last_sweep, (flux_x(v2, H - 1), (zero,) * 6))
    rows = moments.shape[0]
    col = lax.broadcasted_iota(jnp.int32, (rows, 128), 1)
    out = jnp.zeros((rows, 128), F32)
    for k, value in enumerate(acc):
        total = jnp.sum(jnp.sum(value, axis=0, keepdims=True), axis=1, keepdims=True)
        out = jnp.where(col == k, total, out)
    moments[...] = out


def cg_coefficients(mu):
    def form(p, shift):
        total = None
        for i, a in enumerate(p):
            for j, b in enumerate(p):
                term = a * b * mu[i + j + shift]
                total = term if total is None else total + term
        return total

    one = jnp.ones_like(mu[0])
    a0 = mu[0] / mu[1]
    r1 = (one, -a0)
    n1 = form(r1, 0)
    b0 = n1 / mu[0]
    p1 = (one + b0, -a0)
    a1 = n1 / form(p1, 1)
    r2 = (one, r1[1] - a1 * p1[0], -a1 * p1[1])
    n2 = form(r2, 0)
    b1 = n2 / n1
    p2 = (r2[0] + b1 * p1[0], r2[1] + b1 * p1[1], r2[2])
    a2 = n2 / form(p2, 1)
    return (a0 + a1 * p1[0] + a2 * p2[0], a1 * p1[1] + a2 * p2[1], a2 * p2[2])


def step_kernel(moments, pops, mask, pv, v0, v1, v2, xlo, xhi, ylo, yhi,
                potential, nxt, pot, coll):
    nx, _, nz = mask.shape
    top = nx + H
    row = jnp.sum(moments[...], axis=0, keepdims=True)
    col = lax.broadcasted_iota(jnp.int32, (1, 128), 1)
    mu = [jnp.sum(jnp.where(col == k, row, 0.0), axis=1, keepdims=True) for k in range(6)]
    coef = [c * SCALE for c in cg_coefficients(mu)]

    def correct(x, _):
        pot[x] = pv[x] + (coef[0] * v0[x] + coef[1] * v1[x] + coef[2] * v2[x])
        return 0

    lax.fori_loop(H - 2, top + 2, correct, 0)

    lane = lax.broadcasted_iota(jnp.int32, (T, nz), 1)
    line = lax.broadcasted_iota(jnp.int32, (T, nz), 0)

    def moved(species, way, current, density, grad):
        sign = 1.0 if way % 2 == 1 else -1.0
        velocity = sign * (DRIFT_COEF[species] * grad)
        balance = WEIGHTS[way] * density * (1.0 + 4.0 * velocity)
        return current - (1.0 / RELAX_TIME[species]) * (current - balance)

    for species in range(2):
        grad = 0.5 * (pot[H, T:2 * T] - pot[H - 2, T:2 * T])
        coll[species, 1, 0] = moved(species, 1, xlo[POP + species], xlo[DENS + species], grad)
        grad = 0.5 * (pot[top + 1, T:2 * T] - pot[top - 1, T:2 * T])
        coll[species, 2, nx + 1] = moved(species, 2, xhi[POP + species], xhi[DENS + species], grad)

    def collide(x, _):
        at = x + H
        wide = pot[at]
        mid = wide[T:2 * T]
        potential[x] = mid
        gx = 0.5 * (pot[at + 1, T:2 * T] - pot[at - 1, T:2 * T])
        gy = 0.5 * (pltpu.roll(wide, 3 * T - 1, 0)[T:2 * T] - pltpu.roll(wide, 1, 0)[T:2 * T])
        gz = 0.5 * (jnp.where(lane == nz - 1, 0.0, pltpu.roll(mid, nz - 1, 1))
                    - jnp.where(lane == 0, 0.0, pltpu.roll(mid, 1, 1)))
        grads = (None, gx, gx, gy, gy, gz, gz)
        for species in range(2):
            current = [pops[species, i, x] for i in range(7)]
            density = current[0]
            for i in range(1, 7):
                density = density + current[i]
            rate = 1.0 / RELAX_TIME[species]
            coll[species, 0, x + 1] = current[0] - rate * (current[0] - WEIGHTS[0] * density)
            for i in range(1, 7):
                coll[species, i, x + 1] = moved(species, i, current[i], density, grads[i])
        return 0

    lax.fori_loop(0, nx, collide, 0)

    def stream(x, _):
        at = x + H
        solid = mask[x].astype(F32)
        below = jnp.where(x == 0, xlo[SOLID], mask[jnp.maximum(x - 1, 0)].astype(F32))
        above = jnp.where(x == nx - 1, xhi[SOLID], mask[jnp.minimum(x + 1, nx - 1)].astype(F32))
        blocked = (
            None,
            below > 0.5,
            above > 0.5,
            jnp.where(line == 0, ylo[x, SOLID:SOLID + 1], pltpu.roll(solid, 1, 0)) > 0.5,
            jnp.where(line == T - 1, yhi[x, SOLID:SOLID + 1], pltpu.roll(solid, T - 1, 0)) > 0.5,
            jnp.where(lane == 0, 1.0, pltpu.roll(solid, 1, 1)) > 0.5,
            jnp.where(lane == nz - 1, 1.0, pltpu.roll(solid, nz - 1, 1)) > 0.5,
        )
        free = 1.0 - solid
        grad_lo = 0.5 * (pot[at, T:T + 1] - pot[at, T - 2:T - 1])
        grad_hi = 0.5 * (pot[at, 2 * T + 1:2 * T + 2] - pot[at, 2 * T - 1:2 * T])
        for species in range(2):
            c = [None] + [coll[species, i, x + 1] for i in range(1, 7)]
            from_lo = moved(species, 3, ylo[x, POP + species:POP + species + 1],
                            ylo[x, DENS + species:DENS + species + 1], grad_lo)
            from_hi = moved(species, 4, yhi[x, POP + species:POP + species + 1],
                            yhi[x, DENS + species:DENS + species + 1], grad_hi)
            source = (
                None,
                coll[species, 1, x],
                coll[species, 2, x + 2],
                jnp.where(line == 0, from_lo, pltpu.roll(c[3], 1, 0)),
                jnp.where(line == T - 1, from_hi, pltpu.roll(c[4], T - 1, 0)),
                pltpu.roll(c[5], 1, 1),
                pltpu.roll(c[6], nz - 1, 1),
            )
            nxt[species, 0, x] = coll[species, 0, x + 1] * free
            for i in range(1, 7):
                nxt[species, i, x] = jnp.where(blocked[i], c[OPPOSITE[i]], source[i]) * free
        return 0

    lax.fori_loop(0, nx, stream, 0)


def shift(block, axis, distance):
    n = lax.axis_size(axis)
    return lax.ppermute(block, axis, [(i, (i + distance) % n) for i in range(n)])


def local(populations, conductivity, deposit_mask, electrode_flags, previous_potential):
    nx, ny, nz = conductivity.shape
    brick = jax.ShapeDtypeStruct((nx, ny, nz), F32)
    x_face = jax.ShapeDtypeStruct((22, ny, nz), F32)
    y_face = jax.ShapeDtypeStruct((nx, FACE_ROWS, nz), F32)
    charge, sigma, xlo_s, xhi_s, ylo_s, yhi_s = pl.pallas_call(
        pack_kernel,
        out_shape=(brick, brick, x_face, x_face, y_face, y_face),
        in_specs=[VMEM] * 5,
        out_specs=(VMEM,) * 6,
        compiler_params=params(16),
        name="pack",
    )(populations, conductivity, deposit_mask, electrode_flags, previous_potential)
    xlo = shift(xhi_s, "gx", 1)
    xhi = shift(xlo_s, "gx", -1)
    ylo = shift(yhi_s, "gy", 1)
    yhi = shift(ylo_s, "gy", -1)
    corner = jax.ShapeDtypeStruct((8, ny, nz), F32)
    clo_s, chi_s = pl.pallas_call(
        corner_kernel,
        out_shape=(corner, corner),
        in_specs=[VMEM] * 2,
        out_specs=(VMEM,) * 2,
        compiler_params=params(8),
        name="corners",
    )(xlo, xhi)
    clo = shift(chi_s, "gy", 1)
    chi = shift(clo_s, "gy", -1)
    shape = (nx + 2 * H, 3 * T, nz)
    padded = jax.ShapeDtypeStruct(shape, F32)
    count = lax.axis_size("gx") * lax.axis_size("gy")
    pv, v0, v1, v2, moments = pl.pallas_call(
        krylov_kernel,
        out_shape=(padded,) * 4 + (jax.ShapeDtypeStruct((count, 128), F32),),
        in_specs=[VMEM] * 10,
        out_specs=(VMEM,) * 5,
        scratch_shapes=[pltpu.VMEM(shape, F32)] * 6,
        compiler_params=params(24),
        name="krylov",
    )(sigma, charge, electrode_flags, previous_potential, xlo, xhi, ylo, yhi, clo, chi)
    moments = lax.all_to_all(moments, ("gx", "gy"), 0, 0, tiled=True)
    return pl.pallas_call(
        step_kernel,
        out_shape=(brick, jax.ShapeDtypeStruct(populations.shape, F32)),
        in_specs=[VMEM] * 11,
        out_specs=(VMEM,) * 2,
        scratch_shapes=[
            pltpu.VMEM(shape, F32),
            pltpu.VMEM((2, 7, nx + 2, ny, nz), F32),
        ],
        compiler_params=params(28),
        name="step",
    )(moments, populations, deposit_mask, pv, v0, v1, v2, xlo, xhi, ylo, yhi)


def solution(mesh):
    in_specs = (
        P(None, None, "gx", "gy", None),
        P("gx", "gy", None),
        P("gx", "gy", None),
        P("gx", "gy", None),
        P("gx", "gy", None),
    )
    out_specs = (P("gx", "gy", None), P(None, None, "gx", "gy", None))
    return jax.shard_map(local, mesh=mesh, in_specs=in_specs, out_specs=out_specs, check_vma=False)
```

```python
import jax
import jax.numpy as jnp
from jax import lax
from jax.experimental import pallas as pl
from jax.experimental.pallas import tpu as pltpu
from jax.sharding import PartitionSpec as P

SCREEN_RATE = 0.01
WEIGHTS = (0.25, 0.125, 0.125, 0.125, 0.125, 0.125, 0.125)
OPPOSITE = (0, 2, 1, 4, 3, 6, 5)
DRIFT_COEF = (-0.02, 0.016)
RELAX_TIME = (0.8, 1.1)

H = 5
T = 8
SCALE = 0.0625

PREV, SIGMA, FLAGS, CHARGE = (0, 5), (5, 5), (10, 4), (14, 3)
DENS, POP, SOLID = 17, 19, 21
FACE_ROWS = 24

CORNER = (
    ("prev", 1, 4, 0, 0), ("prev", 2, 3, 0, 4), ("prev", 4, 1, 0, 7),
    ("sigma", 1, 4, 1, 0), ("sigma", 2, 3, 1, 4), ("sigma", 4, 1, 1, 7),
    ("prev", 3, 2, 2, 0), ("sigma", 3, 2, 2, 2), ("flags", 2, 2, 2, 4), ("charge", 2, 2, 2, 6),
    ("flags", 1, 3, 3, 0), ("charge", 1, 3, 3, 3), ("flags", 3, 1, 3, 6), ("charge", 3, 1, 3, 7),
)
SPAN = {"prev": PREV, "sigma": SIGMA, "flags": FLAGS, "charge": CHARGE}
VMEM = pl.BlockSpec(memory_space=pltpu.VMEM)
HBM = pl.BlockSpec(memory_space=pltpu.HBM)
F32 = jnp.float32


def params(mib):
    return pltpu.CompilerParams(vmem_limit_bytes=mib * 1024 * 1024)


def load_kernel(pops_hbm, cond_hbm, mask_hbm, flags_hbm, prev_hbm,
                pops, sigma, solid, flags, prev, charge, xlo, xhi, cond, mask, marks, sem):
    nx = sigma.shape[0]
    quarter = nx // 4
    small = [
        pltpu.make_async_copy(src, dst, sem.at[4 + i])
        for i, (src, dst) in enumerate(
            ((cond_hbm, cond), (mask_hbm, mask), (flags_hbm, marks), (prev_hbm, prev))
        )
    ]
    large = [
        pltpu.make_async_copy(
            pops_hbm.at[:, :, pl.ds(q * quarter, quarter)],
            pops.at[:, :, pl.ds(q * quarter, quarter)],
            sem.at[q],
        )
        for q in range(4)
    ]
    for copy in small + large:
        copy.start()
    for copy in small:
        copy.wait()
    for x in range(nx):
        s = mask[x].astype(F32)
        solid[x] = s
        sigma[x] = cond[x] * (1.0 + 3.0 * s)
        flags[x] = marks[x].astype(F32)

    def density(species, x):
        d = pops[species, 0, x]
        for i in range(1, 7):
            d = d + pops[species, i, x]
        return d

    def edge(out, x, way):
        out[DENS] = density(0, x)
        out[DENS + 1] = density(1, x)
        out[POP] = pops[0, way, x]
        out[POP + 1] = pops[1, way, x]
        out[SOLID] = solid[x]

    for q in range(4):
        large[q].wait()
        for x in range(q * quarter, (q + 1) * quarter):
            charge[x] = 2.0 * density(0, x) - 2.0 * density(1, x)
    for out, up, way in ((xlo, False, 2), (xhi, True, 1)):
        def start(n, skip=0):
            return nx - n - skip if up else skip
        for src, (first, n), skip in ((prev, PREV, 0), (sigma, SIGMA, 0), (flags, FLAGS, 0), (charge, CHARGE, 1)):
            out[first:first + n] = src[start(n, skip):start(n, skip) + n]
        edge(out, start(1), way)


def on_parity(run):
    odd = lax.rem(lax.axis_index("gy"), 2)
    pl.when(odd == 0)(lambda: run(1, 0))
    pl.when(odd == 1)(lambda: run(0, 1))


def pack_kernel(pops, sigma, solid, flags, prev, charge, mate, other):
    on_parity(lambda lo, hi: pack_faces(
        pops, sigma, solid, flags, prev, charge, (mate, other)[lo], (mate, other)[hi]))


def pack_faces(pops, sigma, solid, flags, prev, charge, ylo, yhi):
    nx = sigma.shape[0]

    def row(x, _):
        d0, d1 = pops[0, 0, x], pops[1, 0, x]
        for i in range(1, 7):
            d0 = d0 + pops[0, i, x]
            d1 = d1 + pops[1, i, x]
        values = (prev[x], sigma[x], flags[x], charge[x])
        sd = solid[x]
        for out, up, way in ((ylo, False, 4), (yhi, True, 3)):
            def put(first, n, value, skip=0):
                at = T - n - skip if up else skip
                out[x, first:first + n] = value[at:at + n]
            for value, (first, n), skip in zip(values, (PREV, SIGMA, FLAGS, CHARGE), (0, 0, 0, 1)):
                put(first, n, value, skip)
            put(DENS, 1, d0)
            put(DENS + 1, 1, d1)
            put(POP, 1, pops[0, way, x])
            put(POP + 1, 1, pops[1, way, x])
            put(SOLID, 1, sd)
            put(SOLID + 1, 2, sd)
        return 0

    lax.fori_loop(0, nx, row, 0, unroll=4)


def x_row(buf, side, name, distance):
    if name == "charge":
        if distance == 1:
            return 2.0 * buf[DENS] - 2.0 * buf[DENS + 1]
        return buf[CHARGE[0] + (4 - distance if side == 0 else distance - 2)]
    first, n = SPAN[name]
    return buf[first + (n - distance if side == 0 else distance - 1)]


def corner_kernel(xlo, xhi, mate, other):
    on_parity(lambda lo, hi: pack_corners(xlo, xhi, (mate, other)[lo], (mate, other)[hi]))


def pack_corners(xlo, xhi, clo, chi):
    for side, buf in ((0, xlo), (1, xhi)):
        for name, distance, n, tile, at in CORNER:
            value = x_row(buf, side, name, distance)
            clo[4 * side + tile, at:at + n] = value[:n]
            chi[4 * side + tile, at:at + n] = value[T - n:]


def harmonic(a, b):
    return 2.0 * a * b / (a + b)


def laplace(m, above, below_flux, wx, wy, wz, sg, first, last):
    nz = m.shape[1]
    fx = wx * (m - above)
    fy = wy * (m - pltpu.roll(m, 3 * T - 1, 0))
    fz = wz * (m - jnp.where(last, 0.0, pltpu.roll(m, nz - 1, 1)))
    s = fx - below_flux
    s = s + (fy - pltpu.roll(fy, 1, 0))
    s = s + (fz + jnp.where(first, sg * m, -pltpu.roll(fz, 1, 1)))
    return s + SCREEN_RATE * m, fx


def mapped(u, value, v):
    return (u * value + (1.0 - u) * v) * SCALE


def ends(nz):
    lane = lax.broadcasted_iota(jnp.int32, (3 * T, nz), 1)
    return lane == 0, lane == nz - 1


def dots(a, b, c, d):
    return (a * a, a * b, b * b, b * c, c * c, c * d)


def place_faces(sigma, charge, flags, prev, ylo, yhi, pv, sg, un, ch, rest_lo, rest_hi):
    nx = sigma.shape[0]

    def own(x, _):
        at = x + H
        pv[at, T:2 * T] = prev[x]
        sg[at, T:2 * T] = sigma[x]
        un[at, T:2 * T] = 1.0 - flags[x]
        ch[at, T:2 * T] = charge[x]
        for buf, up, rest in ((ylo, False, rest_lo), (yhi, True, rest_hi)):
            rest[x] = buf[x, 2 * T:3 * T]
            def put(ref, first, n, skip=0, one=False):
                to = 2 * T + skip if up else T - n - skip
                value = buf[x, first:first + n]
                ref[at, to:to + n] = 1.0 - value if one else value
            put(pv, *PREV)
            put(sg, *SIGMA)
            put(un, *FLAGS, 0, True)
            put(ch, *CHARGE, 1)
            to = 2 * T if up else T - 1
            ch[at, to:to + 1] = 2.0 * buf[x, DENS:DENS + 1] - 2.0 * buf[x, DENS + 1:DENS + 2]
        return 0

    lax.fori_loop(0, nx, own, 0, unroll=4)


def inner_kernel(sigma, charge, flags, prev, mate, other,
                 pv, sg, un, wx, wy, wz, v0, v1, v2, ch, sums, rest_lo, rest_hi):
    nx, _, nz = sigma.shape
    top = nx + H
    first, last = ends(nz)
    on_parity(lambda lo, hi: place_faces(
        sigma, charge, flags, prev, (mate, other)[lo], (mate, other)[hi], pv, sg, un, ch, rest_lo, rest_hi))

    def faces(x, a):
        b = sg[jnp.minimum(x + 1, top - 1)]
        wx[x] = harmonic(a, b)
        wy[x] = harmonic(a, pltpu.roll(a, 3 * T - 1, 0))
        wz[x] = harmonic(a, jnp.where(last, a, pltpu.roll(a, nz - 1, 1)))
        return b

    lax.fori_loop(H, top, faces, sg[H], unroll=4)

    def sweep(src, lo, hi, store, unroll):
        def body(x, below):
            value, below = laplace(src[x], src[x + 1], below, wx[x], wy[x], wz[x], sg[x], first, last)
            store(x, value)
            return below
        lax.fori_loop(lo, hi, body, wx[lo - 1] * (src[lo - 1] - src[lo]), unroll=unroll)

    def store_v0(x, value):
        v0[x] = un[x] * (ch[x] - value)

    def apply_to(src, dst):
        def store(x, value):
            dst[x] = mapped(un[x], value, src[x])
        return store

    sweep(pv, H + 1, top - 1, store_v0, 7)
    sweep(v0, H + 2, top - 2, apply_to(v0, v1), 6)
    sweep(v1, H + 3, top - 3, apply_to(v1, v2), 5)

    def last_sweep(x, carry):
        below, acc = carry
        value, below = laplace(v2[x], v2[x + 1], below, wx[x], wy[x], wz[x], sg[x], first, last)
        a, b, c = v0[x, T:2 * T], v1[x, T:2 * T], v2[x, T:2 * T]
        d = mapped(un[x, T:2 * T], value[T:2 * T], c)
        return below, tuple(s + t for s, t in zip(acc, dots(a, b, c, d)))

    zero = jnp.zeros((T, nz), F32)
    below = wx[H + 3] * (v2[H + 3] - v2[H + 4])
    _, acc = lax.fori_loop(H + 4, top - 4, last_sweep, (below, (zero,) * 6), unroll=4)
    for k, value in enumerate(acc):
        sums[k] = value


def outer_kernel(pv_in, sg_in, un_in, wx_in, wy_in, wz_in, v0_in, v1_in, v2_in, ch_in, sums,
                 xlo, xhi, mate, other,
                 pv_out, v0_out, v1_out, v2_out, moments, sg_out, un_out, ch_out, wx_out, wy_out, wz_out):
    nx, nz = pv_in.shape[0] - 2 * H, pv_in.shape[2]
    top = nx + H
    first, last = ends(nz)

    def outer(x):
        return x if x < 8 else x - (nx + 2 * H - 16)

    class Rows:
        def __init__(self, inner, out, lo, hi):
            self.inner, self.out, self.lo, self.hi = inner, out, lo, hi

        def __getitem__(self, x):
            return self.inner[x] if self.lo <= x < self.hi else self.out[outer(x)]

        def own(self, x):
            if self.lo <= x < self.hi:
                return self.inner[x, T:2 * T]
            return self.out[outer(x), T:2 * T]

        def __setitem__(self, x, value):
            self.out[outer(x)] = value

    pv, sg, un = Rows(pv_in, pv_out, H, top), Rows(sg_in, sg_out, H, top), Rows(un_in, un_out, H, top)
    wx, wy, wz = Rows(wx_in, wx_out, H, top - 1), Rows(wy_in, wy_out, H, top), Rows(wz_in, wz_out, H, top)
    v0, v1, v2 = Rows(v0_in, v0_out, H + 1, top - 1), Rows(v1_in, v1_out, H + 2, top - 2), Rows(v2_in, v2_out, H + 3, top - 3)

    ch = Rows(ch_in, ch_out, H, top)

    def row_at(side, distance):
        return outer(H - distance if side == 0 else top - 1 + distance)

    for side, buf in ((0, xlo), (1, xhi)):
        for distance in range(1, 6):
            at = row_at(side, distance)
            pv_out[at, T:2 * T] = x_row(buf, side, "prev", distance)
            sg_out[at, T:2 * T] = x_row(buf, side, "sigma", distance)
            if distance < 5:
                un_out[at, T:2 * T] = 1.0 - x_row(buf, side, "flags", distance)
                ch_out[at, T:2 * T] = x_row(buf, side, "charge", distance)

    def place_corners(lo, hi):
        for side in range(2):
            for name, distance, n, tile, row in CORNER:
                ref = {"prev": pv_out, "sigma": sg_out, "flags": un_out, "charge": ch_out}[name]
                for buf, to in (((mate, other)[lo], T - n), ((mate, other)[hi], 2 * T)):
                    value = buf[4 * side + tile, row:row + n]
                    ref[row_at(side, distance), to:to + n] = 1.0 - value if name == "flags" else value

    on_parity(place_corners)
    low, high = range(0, H), range(top - 1, top + H)
    for x in (*low, *high):
        a = sg[x]
        if x < top + H - 1:
            wx[x] = harmonic(a, sg[x + 1])
        if 0 < x < top + H - 1 and x != top - 1:
            wy[x] = harmonic(a, pltpu.roll(a, 3 * T - 1, 0))
            wz[x] = harmonic(a, jnp.where(last, a, pltpu.roll(a, nz - 1, 1)))

    def sweep(src, margin, store):
        for lo, hi in ((1 + margin, H + 1 + margin), (top - 1 - margin, top + 4 - margin)):
            below = wx[lo - 1] * (src[lo - 1] - src[lo])
            for x in range(lo, hi):
                value, below = laplace(src[x], src[x + 1], below, wx[x], wy[x], wz[x], sg[x], first, last)
                store(x, value)

    def store_v0(x, value):
        v0[x] = un[x] * (ch[x] - value)

    def apply_to(src, dst):
        def store(x, value):
            dst[x] = mapped(un[x], value, src[x])
        return store

    sweep(pv, 0, store_v0)
    sweep(v0, 1, apply_to(v0, v1))
    sweep(v1, 2, apply_to(v1, v2))
    acc = [sums[k] for k in range(6)]
    for lo, hi in ((H, H + 4), (top - 4, top)):
        below = wx[lo - 1] * (v2[lo - 1] - v2[lo])
        for x in range(lo, hi):
            value, below = laplace(v2[x], v2[x + 1], below, wx[x], wy[x], wz[x], sg[x], first, last)
            c = v2.own(x)
            d = mapped(un.own(x), value[T:2 * T], c)
            for k, term in enumerate(dots(v0.own(x), v1.own(x), c, d)):
                acc[k] = acc[k] + term
    rows = moments.shape[0]
    col = lax.broadcasted_iota(jnp.int32, (1, 128), 1)
    line = jnp.zeros((1, 128), F32)
    for k, value in enumerate(acc):
        total = jnp.sum(jnp.sum(value, axis=0, keepdims=True), axis=1, keepdims=True)
        line = jnp.where(col == k, total, line)
    moments[...] = jnp.broadcast_to(line, (rows, 128))


def cg_coefficients(mu):
    def form(p, shift):
        total = None
        for i, a in enumerate(p):
            for j, b in enumerate(p):
                term = a * b * mu[i + j + shift]
                total = term if total is None else total + term
        return total

    one = jnp.ones_like(mu[0])
    a0 = mu[0] / mu[1]
    r1 = (one, -a0)
    n1 = form(r1, 0)
    b0 = n1 / mu[0]
    p1 = (one + b0, -a0)
    a1 = n1 / form(p1, 1)
    r2 = (one, r1[1] - a1 * p1[0], -a1 * p1[1])
    n2 = form(r2, 0)
    b1 = n2 / n1
    p2 = (r2[0] + b1 * p1[0], r2[1] + b1 * p1[1], r2[2])
    a2 = n2 / form(p2, 1)
    return (a0 + a1 * p1[0] + a2 * p2[0], a1 * p1[1] + a2 * p2[1], a2 * p2[2])


def step_kernel(moments, pops, solids, pv, v0, v1, v2, pv_x, v0_x, v1_x, v2_x, xlo, xhi, ylo, yhi,
                potential_hbm, nxt_hbm, pot, coll, nxt, potential, sem):
    nx, _, nz = solids.shape
    top = nx + H
    row = jnp.sum(moments[...], axis=0, keepdims=True)
    col = lax.broadcasted_iota(jnp.int32, (1, 128), 1)
    mu = [jnp.sum(jnp.where(col == k, row, 0.0), axis=1, keepdims=True) for k in range(6)]
    coef = [c * SCALE for c in cg_coefficients(mu)]

    def corrected(p, a, b, c):
        return p + (coef[0] * a + coef[1] * b + coef[2] * c)

    def correct(x, _):
        pot[x] = corrected(pv[x], v0[x], v1[x], v2[x])
        return 0

    lax.fori_loop(H + 3, top - 3, correct, 0, unroll=5)
    for x in (*range(H - 2, H + 3), *range(top - 3, top + 2)):
        depth = min(x - H, top - 1 - x)
        out = x if x < 8 else x - (nx + 2 * H - 16)
        pot[x] = corrected(
            pv[x] if depth >= 0 else pv_x[out],
            v0[x] if depth >= 1 else v0_x[out],
            v1[x] if depth >= 2 else v1_x[out],
            v2_x[out],
        )

    lane = lax.broadcasted_iota(jnp.int32, (T, nz), 1)
    line = lax.broadcasted_iota(jnp.int32, (T, nz), 0)

    def moved(species, way, current, density, grad):
        sign = 1.0 if way % 2 == 1 else -1.0
        velocity = sign * (DRIFT_COEF[species] * grad)
        balance = WEIGHTS[way] * density * (1.0 + 4.0 * velocity)
        return current - (1.0 / RELAX_TIME[species]) * (current - balance)

    for species in range(2):
        grad = 0.5 * (pot[H, T:2 * T] - pot[H - 2, T:2 * T])
        coll[species, 1, 0] = moved(species, 1, xlo[POP + species], xlo[DENS + species], grad)
        grad = 0.5 * (pot[top + 1, T:2 * T] - pot[top - 1, T:2 * T])
        coll[species, 2, nx + 1] = moved(species, 2, xhi[POP + species], xhi[DENS + species], grad)

    def collide(x):
        at = x + H
        wide = pot[at]
        mid = wide[T:2 * T]
        potential[x] = mid
        gx = 0.5 * (pot[at + 1, T:2 * T] - pot[at - 1, T:2 * T])
        gy = 0.5 * (pltpu.roll(wide, 3 * T - 1, 0)[T:2 * T] - pltpu.roll(wide, 1, 0)[T:2 * T])
        gz = 0.5 * (jnp.where(lane == nz - 1, 0.0, pltpu.roll(mid, nz - 1, 1))
                    - jnp.where(lane == 0, 0.0, pltpu.roll(mid, 1, 1)))
        grads = (None, gx, gx, gy, gy, gz, gz)
        for species in range(2):
            current = [pops[species, i, x] for i in range(7)]
            density = current[0]
            for i in range(1, 7):
                density = density + current[i]
            rate = 1.0 / RELAX_TIME[species]
            coll[species, 0, x + 1] = current[0] - rate * (current[0] - WEIGHTS[0] * density)
            for i in range(1, 7):
                coll[species, i, x + 1] = moved(species, i, current[i], density, grads[i])

    def stream(x):
        at = x + H
        solid = solids[x]
        below = jnp.where(x == 0, xlo[SOLID], solids[jnp.maximum(x - 1, 0)])
        above = jnp.where(x == nx - 1, xhi[SOLID], solids[jnp.minimum(x + 1, nx - 1)])
        blocked = (
            None,
            below > 0.5,
            above > 0.5,
            jnp.where(line == 0, ylo[x, SOLID - 2 * T:SOLID - 2 * T + 1], pltpu.roll(solid, 1, 0)) > 0.5,
            jnp.where(line == T - 1, yhi[x, SOLID - 2 * T:SOLID - 2 * T + 1], pltpu.roll(solid, T - 1, 0)) > 0.5,
            jnp.where(lane == 0, 1.0, pltpu.roll(solid, 1, 1)) > 0.5,
            jnp.where(lane == nz - 1, 1.0, pltpu.roll(solid, nz - 1, 1)) > 0.5,
        )
        free = 1.0 - solid
        grad_lo = 0.5 * (pot[at, T:T + 1] - pot[at, T - 2:T - 1])
        grad_hi = 0.5 * (pot[at, 2 * T + 1:2 * T + 2] - pot[at, 2 * T - 1:2 * T])
        for species in range(2):
            c = [None] + [coll[species, i, x + 1] for i in range(1, 7)]
            from_lo = moved(species, 3, ylo[x, POP - 2 * T + species:POP - 2 * T + species + 1],
                            ylo[x, DENS - 2 * T + species:DENS - 2 * T + species + 1], grad_lo)
            from_hi = moved(species, 4, yhi[x, POP - 2 * T + species:POP - 2 * T + species + 1],
                            yhi[x, DENS - 2 * T + species:DENS - 2 * T + species + 1], grad_hi)
            source = (
                None,
                coll[species, 1, x],
                coll[species, 2, x + 2],
                jnp.where(line == 0, from_lo, pltpu.roll(c[3], 1, 0)),
                jnp.where(line == T - 1, from_hi, pltpu.roll(c[4], T - 1, 0)),
                pltpu.roll(c[5], 1, 1),
                pltpu.roll(c[6], nz - 1, 1),
            )
            nxt[species, 0, x] = coll[species, 0, x + 1] * free
            for i in range(1, 7):
                nxt[species, i, x] = jnp.where(blocked[i], c[OPPOSITE[i]], source[i]) * free

    def both(x, _):
        collide(x + 1)
        stream(x)
        return 0

    collide(0)
    quarter = nx // 4
    copies = []
    for q in range(4):
        end = (q + 1) * quarter
        lax.fori_loop(q * quarter, min(end, nx - 1), both, 0)
        if end == nx:
            stream(nx - 1)
        rows = pl.ds(q * quarter, quarter)
        copies.append(pltpu.make_async_copy(nxt.at[:, :, rows], nxt_hbm.at[:, :, rows], sem.at[q]))
        copies[-1].start()
        if end == nx:
            copies.append(pltpu.make_async_copy(potential, potential_hbm, sem.at[4]))
            copies[-1].start()
    for copy in copies:
        copy.wait()


def to_mate(block):
    n = lax.axis_size("gy")
    return lax.ppermute(block, "gy", [(i, i ^ 1) for i in range(n)])


def to_other(block):
    n = lax.axis_size("gy")
    return lax.ppermute(block, "gy", [(i, (i + (1 if i % 2 else -1)) % n) for i in range(n)])


def shift(block, axis, distance):
    n = lax.axis_size(axis)
    return lax.ppermute(block, axis, [(i, (i + distance) % n) for i in range(n)])


def local(populations, conductivity, deposit_mask, electrode_flags, previous_potential):
    nx, ny, nz = conductivity.shape
    brick = jax.ShapeDtypeStruct((nx, ny, nz), F32)
    x_face = jax.ShapeDtypeStruct((22, ny, nz), F32)
    y_face = jax.ShapeDtypeStruct((nx, FACE_ROWS, nz), F32)
    whole = jax.ShapeDtypeStruct(populations.shape, F32)
    pops, sigma, solid, flags, prev, charge, xlo_s, xhi_s = pl.pallas_call(
        load_kernel,
        out_shape=(whole, brick, brick, brick, brick, brick, x_face, x_face),
        in_specs=[HBM] * 5,
        out_specs=(VMEM,) * 8,
        scratch_shapes=[
            pltpu.VMEM(conductivity.shape, F32),
            pltpu.VMEM(conductivity.shape, jnp.int32),
            pltpu.VMEM(conductivity.shape, jnp.int32),
            pltpu.SemaphoreType.DMA((8,)),
        ],
        compiler_params=params(16),
        name="load",
    )(*(pltpu.with_memory_space_constraint(a, pltpu.HBM) for a in (
        populations, conductivity, deposit_mask, electrode_flags, previous_potential)))
    xlo = shift(xhi_s, "gx", 1)
    xhi = shift(xlo_s, "gx", -1)
    y_mate, y_other = pl.pallas_call(
        pack_kernel,
        out_shape=(y_face, y_face),
        in_specs=[VMEM] * 6,
        out_specs=(VMEM,) * 2,
        compiler_params=params(16),
        name="pack",
    )(pops, sigma, solid, flags, prev, charge)
    y_mate = to_mate(y_mate)
    y_other = to_other(y_other)
    corner = jax.ShapeDtypeStruct((8, ny, nz), F32)
    c_mate, c_other = pl.pallas_call(
        corner_kernel,
        out_shape=(corner, corner),
        in_specs=[VMEM] * 2,
        out_specs=(VMEM,) * 2,
        compiler_params=params(8),
        name="corners",
    )(xlo, xhi)
    c_mate = to_mate(c_mate)
    c_other = to_other(c_other)
    shape = (nx + 2 * H, 3 * T, nz)
    padded = jax.ShapeDtypeStruct(shape, F32)
    *inner, rest_lo, rest_hi = pl.pallas_call(
        inner_kernel,
        out_shape=(padded,) * 10 + (jax.ShapeDtypeStruct((6, ny, nz), F32), brick, brick),
        in_specs=[VMEM] * 6,
        out_specs=(VMEM,) * 13,
        compiler_params=params(24),
        cost_estimate=pl.CostEstimate(flops=60_000_000, bytes_accessed=20_000_000, transcendentals=0),
        name="inner",
    )(sigma, charge, flags, prev, y_mate, y_other)
    outer_shape = (16, 3 * T, nz)
    edges = jax.ShapeDtypeStruct(outer_shape, F32)
    count = lax.axis_size("gx") * lax.axis_size("gy")
    pv_x, v0_x, v1_x, v2_x, moments = pl.pallas_call(
        outer_kernel,
        out_shape=(edges,) * 4 + (jax.ShapeDtypeStruct((count, 128), F32),),
        in_specs=[VMEM] * 15,
        out_specs=(VMEM,) * 5,
        scratch_shapes=[pltpu.VMEM(outer_shape, F32)] * 6,
        compiler_params=params(28),
        name="outer",
    )(*inner, xlo, xhi, c_mate, c_other)
    moments = lax.all_to_all(moments, ("gx", "gy"), 0, 0, tiled=True)
    pv, v0, v1, v2 = (inner[i] for i in (0, 6, 7, 8))
    return pl.pallas_call(
        step_kernel,
        out_shape=(brick, whole),
        in_specs=[VMEM] * 15,
        out_specs=(HBM,) * 2,
        scratch_shapes=[
            pltpu.VMEM(shape, F32),
            pltpu.VMEM((2, 7, nx + 2, ny, nz), F32),
            pltpu.VMEM(populations.shape, F32),
            pltpu.VMEM(conductivity.shape, F32),
            pltpu.SemaphoreType.DMA((5,)),
        ],
        compiler_params=params(28),
        name="step",
    )(moments, pops, solid, pv, v0, v1, v2, pv_x, v0_x, v1_x, v2_x, xlo, xhi, rest_lo, rest_hi)


def solution(mesh):
    in_specs = (
        P(None, None, "gx", "gy", None),
        P("gx", "gy", None),
        P("gx", "gy", None),
        P("gx", "gy", None),
        P("gx", "gy", None),
    )
    out_specs = (P("gx", "gy", None), P(None, None, "gx", "gy", None))
    return jax.shard_map(local, mesh=mesh, in_specs=in_specs, out_specs=out_specs, check_vma=False)
```

```python
import jax
import jax.numpy as jnp
from jax import lax
from jax.experimental import pallas as pl
from jax.experimental.pallas import tpu as pltpu
from jax.sharding import PartitionSpec as P

SCREEN_RATE = 0.01
WEIGHTS = (0.25, 0.125, 0.125, 0.125, 0.125, 0.125, 0.125)
OPPOSITE = (0, 2, 1, 4, 3, 6, 5)
DRIFT_COEF = (-0.02, 0.016)
RELAX_TIME = (0.8, 1.1)

H = 5
T = 8
SCALE = 0.0625

PREV, SIGMA, FLAGS, CHARGE = (0, 5), (5, 5), (10, 4), (14, 3)
DENS, POP, SOLID = 17, 19, 21
FACE_ROWS = 24

CORNER = (
    ("prev", 1, 4, 0, 0), ("prev", 2, 3, 0, 4), ("prev", 4, 1, 0, 7),
    ("sigma", 1, 4, 1, 0), ("sigma", 2, 3, 1, 4), ("sigma", 4, 1, 1, 7),
    ("prev", 3, 2, 2, 0), ("sigma", 3, 2, 2, 2), ("flags", 2, 2, 2, 4), ("charge", 2, 2, 2, 6),
    ("flags", 1, 3, 3, 0), ("charge", 1, 3, 3, 3), ("flags", 3, 1, 3, 6), ("charge", 3, 1, 3, 7),
)
SPAN = {"prev": PREV, "sigma": SIGMA, "flags": FLAGS, "charge": CHARGE}
VMEM = pl.BlockSpec(memory_space=pltpu.VMEM)
HBM = pl.BlockSpec(memory_space=pltpu.HBM)
F32 = jnp.float32


def params(mib):
    return pltpu.CompilerParams(vmem_limit_bytes=mib * 1024 * 1024)


def density(pops, species, x):
    d = pops[species, 0, x]
    for i in range(1, 7):
        d = d + pops[species, i, x]
    return d


def on_parity(run):
    odd = lax.rem(lax.axis_index("gy"), 2)
    pl.when(odd == 0)(lambda: run(1, 0))
    pl.when(odd == 1)(lambda: run(0, 1))


def load_kernel(pops_hbm, cond_hbm, mask_hbm, flags_hbm, prev_hbm,
                pops, sigma, solid, flags, prev, charge, xlo, xhi, mate, other, cond, mask, marks, sem):
    nx = sigma.shape[0]
    quarter = nx // 4
    small = [
        pltpu.make_async_copy(src, dst, sem.at[4 + i])
        for i, (src, dst) in enumerate(
            ((cond_hbm, cond), (mask_hbm, mask), (flags_hbm, marks), (prev_hbm, prev))
        )
    ]
    large = [
        pltpu.make_async_copy(
            pops_hbm.at[:, :, pl.ds(q * quarter, quarter)],
            pops.at[:, :, pl.ds(q * quarter, quarter)],
            sem.at[q],
        )
        for q in range(4)
    ]
    for copy in small + large:
        copy.start()
    for copy in small:
        copy.wait()
    for x in range(nx):
        s = mask[x].astype(F32)
        solid[x] = s
        sigma[x] = cond[x] * (1.0 + 3.0 * s)
        flags[x] = marks[x].astype(F32)
    for out, up in ((xlo, False), (xhi, True)):
        for src, (first, n) in ((prev, PREV), (sigma, SIGMA), (flags, FLAGS)):
            at = nx - n if up else 0
            out[first:first + n] = src[at:at + n]
    for q in range(4):
        large[q].wait()
        rows = range(q * quarter, (q + 1) * quarter)
        on_parity(lambda lo, hi: pack_faces(
            pops, sigma, solid, flags, prev, charge, (mate, other)[lo], (mate, other)[hi], rows))
        if q in (0, 3):
            out, up, way = (xlo, False, 2) if q == 0 else (xhi, True, 1)
            first, n = CHARGE
            at = nx - n - 1 if up else 1
            out[first:first + n] = charge[at:at + n]
            edge = nx - 1 if up else 0
            for species in range(2):
                out[DENS + species] = density(pops, species, edge)
                out[POP + species] = pops[species, way, edge]
            out[SOLID] = solid[edge]


def pack_faces(pops, sigma, solid, flags, prev, charge, ylo, yhi, rows):
    for x in rows:
        d = (density(pops, 0, x), density(pops, 1, x))
        ch = 2.0 * d[0] - 2.0 * d[1]
        charge[x] = ch
        values = (prev[x], sigma[x], flags[x], ch)
        for out, up, way in ((ylo, False, 4), (yhi, True, 3)):
            def put(first, n, value, skip=0):
                at = T - n - skip if up else skip
                out[x, first:first + n] = value[at:at + n]
            for value, (first, n), skip in zip(values, (PREV, SIGMA, FLAGS, CHARGE), (0, 0, 0, 1)):
                put(first, n, value, skip)
            for species in range(2):
                put(DENS + species, 1, d[species])
                put(POP + species, 1, pops[species, way, x])
            put(SOLID, 1, solid[x])
            put(SOLID + 1, 2, solid[x])


def at_rest(species, way, current, dens):
    return current - (1.0 / RELAX_TIME[species]) * (current - WEIGHTS[way] * dens)


def response(species, dens):
    return (0.5 * 4.0 * WEIGHTS[1] * DRIFT_COEF[species] / RELAX_TIME[species]) * dens


def prepare_kernel(pops, solids, base, gain, blocks, rest, resp):
    nx, _, nz = solids.shape
    lane = lax.broadcasted_iota(jnp.int32, (T, nz), 1)
    line = lax.broadcasted_iota(jnp.int32, (T, nz), 0)
    for x in range(nx):
        for species in range(2):
            dens = density(pops, species, x)
            resp[species, x] = response(species, dens)
            for i in range(7):
                rest[species, i, x] = at_rest(species, i, pops[species, i, x], dens)
    shifts = (None, None, None, (1, 0, line == 0), (T - 1, 0, line == T - 1),
              (1, 1, lane == 0), (nz - 1, 1, lane == nz - 1))
    for x in range(nx):
        solid = solids[x]
        free = 1.0 - solid
        for i in range(1, 7):
            sign = 1.0 if i % 2 == 1 else -1.0
            opposite = OPPOSITE[i]
            if i < 3:
                source = x - 1 if i == 1 else x + 1
                inside = 0 <= source < nx
                block = solids[source] if inside else jnp.ones_like(solid)

                def moved(value, index):
                    return value[(*index, source)]
            else:
                by, axis, border = shifts[i]
                inside = True
                block = jnp.where(border, 1.0, pltpu.roll(solid, by, axis))

                def moved(value, index):
                    return pltpu.roll(value[(*index, x)], by, axis)
            blocks[i - 1, x] = block
            for species in range(2):
                own, back = rest[species, opposite, x], resp[species, x]
                if inside:
                    own = jnp.where(block > 0.5, own, moved(rest, (species, i)))
                    back = jnp.where(block > 0.5, -back, moved(resp, (species,)))
                else:
                    back = -back
                base[species, i, x] = free * own
                gain[species, i - 1, x] = (sign * free) * back
        for species in range(2):
            base[species, 0, x] = free * rest[species, 0, x]


def x_row(buf, side, name, distance):
    if name == "charge":
        if distance == 1:
            return 2.0 * buf[DENS] - 2.0 * buf[DENS + 1]
        return buf[CHARGE[0] + (4 - distance if side == 0 else distance - 2)]
    first, n = SPAN[name]
    return buf[first + (n - distance if side == 0 else distance - 1)]


def corner_kernel(xlo, xhi, blocks, mate, other):
    on_parity(lambda lo, hi: pack_corners(xlo, xhi, (mate, other)[lo], (mate, other)[hi]))


def pack_corners(xlo, xhi, clo, chi):
    for side, buf in ((0, xlo), (1, xhi)):
        for name, distance, n, tile, at in CORNER:
            value = x_row(buf, side, name, distance)
            clo[4 * side + tile, at:at + n] = value[:n]
            chi[4 * side + tile, at:at + n] = value[T - n:]


def harmonic(a, b):
    return 2.0 * a * b / (a + b)


def laplace(m, above, below_flux, wx, wy, wz, sg, first, last):
    nz = m.shape[1]
    fx = wx * (m - above)
    fy = wy * (m - pltpu.roll(m, 3 * T - 1, 0))
    fz = wz * (m - jnp.where(last, 0.0, pltpu.roll(m, nz - 1, 1)))
    s = fx - below_flux
    s = s + (fy - pltpu.roll(fy, 1, 0))
    s = s + (fz + jnp.where(first, sg * m, -pltpu.roll(fz, 1, 1)))
    return s + SCREEN_RATE * m, fx


def mapped(u, value, v):
    return (u * value + (1.0 - u) * v) * SCALE


def ends(nz):
    lane = lax.broadcasted_iota(jnp.int32, (3 * T, nz), 1)
    return lane == 0, lane == nz - 1


def dots(a, b, c, d):
    return (a * a, a * b, b * b, b * c, c * c, c * d)


def place_faces(sigma, charge, flags, prev, ylo, yhi, pv, sg, un, ch, rest_lo, rest_hi):
    nx = sigma.shape[0]

    def own(x, _):
        at = x + H
        pv[at, T:2 * T] = prev[x]
        sg[at, T:2 * T] = sigma[x]
        un[at, T:2 * T] = 1.0 - flags[x]
        ch[at, T:2 * T] = charge[x]
        for buf, up, rest in ((ylo, False, rest_lo), (yhi, True, rest_hi)):
            rest[x] = buf[x, 2 * T:3 * T]
            def put(ref, first, n, skip=0, one=False):
                to = 2 * T + skip if up else T - n - skip
                value = buf[x, first:first + n]
                ref[at, to:to + n] = 1.0 - value if one else value
            put(pv, *PREV)
            put(sg, *SIGMA)
            put(un, *FLAGS, 0, True)
            put(ch, *CHARGE, 1)
            to = 2 * T if up else T - 1
            ch[at, to:to + 1] = 2.0 * buf[x, DENS:DENS + 1] - 2.0 * buf[x, DENS + 1:DENS + 2]
        return 0

    lax.fori_loop(0, nx, own, 0, unroll=4)


def start_kernel(sigma, charge, flags, prev, mate, other,
                 pv, sg, un, wx, wy, wz, v0, ch, rest_lo, rest_hi):
    nx, _, nz = sigma.shape
    top = nx + H
    first, last = ends(nz)
    on_parity(lambda lo, hi: place_faces(
        sigma, charge, flags, prev, (mate, other)[lo], (mate, other)[hi], pv, sg, un, ch, rest_lo, rest_hi))

    def faces(x, a):
        b = sg[jnp.minimum(x + 1, top - 1)]
        wx[x] = harmonic(a, b)
        wy[x] = harmonic(a, pltpu.roll(a, 3 * T - 1, 0))
        wz[x] = harmonic(a, jnp.where(last, a, pltpu.roll(a, nz - 1, 1)))
        return b

    lax.fori_loop(H, top, faces, sg[H], unroll=4)

    def store_v0(x, value):
        v0[x] = un[x] * (ch[x] - value)

    inner_sweep(pv, H + 1, top - 1, store_v0, 7, wx, wy, wz, sg)


def inner_sweep(src, lo, hi, store, unroll, wx, wy, wz, sg):
    first, last = ends(src.shape[2])

    def body(x, below):
        value, below = laplace(src[x], src[x + 1], below, wx[x], wy[x], wz[x], sg[x], first, last)
        store(x, value)
        return below

    lax.fori_loop(lo, hi, body, wx[lo - 1] * (src[lo - 1] - src[lo]), unroll=unroll)


def inner_kernel(sg, un, wx, wy, wz, v0, v1, v2, sums):
    nx, nz = sg.shape[0] - 2 * H, sg.shape[2]
    top = nx + H
    first, last = ends(nz)

    def apply_to(src, dst):
        def store(x, value):
            dst[x] = mapped(un[x], value, src[x])
        return store

    inner_sweep(v0, H + 2, top - 2, apply_to(v0, v1), 6, wx, wy, wz, sg)
    inner_sweep(v1, H + 3, top - 3, apply_to(v1, v2), 5, wx, wy, wz, sg)

    def last_sweep(x, carry):
        below, acc = carry
        value, below = laplace(v2[x], v2[x + 1], below, wx[x], wy[x], wz[x], sg[x], first, last)
        a, b, c = v0[x, T:2 * T], v1[x, T:2 * T], v2[x, T:2 * T]
        d = mapped(un[x, T:2 * T], value[T:2 * T], c)
        return below, tuple(s + t for s, t in zip(acc, dots(a, b, c, d)))

    zero = jnp.zeros((T, nz), F32)
    below = wx[H + 3] * (v2[H + 3] - v2[H + 4])
    _, acc = lax.fori_loop(H + 4, top - 4, last_sweep, (below, (zero,) * 6), unroll=4)
    for k, value in enumerate(acc):
        sums[k] = value


def outer_kernel(pv_in, sg_in, un_in, wx_in, wy_in, wz_in, v0_in, ch_in, v1_in, v2_in, sums,
                 xlo, xhi, mate, other,
                 pv_out, v0_out, v1_out, v2_out, moments, sg_out, un_out, ch_out, wx_out, wy_out, wz_out):
    nx, nz = pv_in.shape[0] - 2 * H, pv_in.shape[2]
    top = nx + H
    first, last = ends(nz)

    def outer(x):
        return x if x < 8 else x - (nx + 2 * H - 16)

    class Rows:
        def __init__(self, inner, out, lo, hi):
            self.inner, self.out, self.lo, self.hi = inner, out, lo, hi

        def __getitem__(self, x):
            return self.inner[x] if self.lo <= x < self.hi else self.out[outer(x)]

        def own(self, x):
            if self.lo <= x < self.hi:
                return self.inner[x, T:2 * T]
            return self.out[outer(x), T:2 * T]

        def __setitem__(self, x, value):
            self.out[outer(x)] = value

    pv, sg, un = Rows(pv_in, pv_out, H, top), Rows(sg_in, sg_out, H, top), Rows(un_in, un_out, H, top)
    wx, wy, wz = Rows(wx_in, wx_out, H, top - 1), Rows(wy_in, wy_out, H, top), Rows(wz_in, wz_out, H, top)
    v0, v1, v2 = Rows(v0_in, v0_out, H + 1, top - 1), Rows(v1_in, v1_out, H + 2, top - 2), Rows(v2_in, v2_out, H + 3, top - 3)

    ch = Rows(ch_in, ch_out, H, top)

    def row_at(side, distance):
        return outer(H - distance if side == 0 else top - 1 + distance)

    for side, buf in ((0, xlo), (1, xhi)):
        for distance in range(1, 6):
            at = row_at(side, distance)
            pv_out[at, T:2 * T] = x_row(buf, side, "prev", distance)
            sg_out[at, T:2 * T] = x_row(buf, side, "sigma", distance)
            if distance < 5:
                un_out[at, T:2 * T] = 1.0 - x_row(buf, side, "flags", distance)
                ch_out[at, T:2 * T] = x_row(buf, side, "charge", distance)

    def place_corners(lo, hi):
        for side in range(2):
            for name, distance, n, tile, row in CORNER:
                ref = {"prev": pv_out, "sigma": sg_out, "flags": un_out, "charge": ch_out}[name]
                for buf, to in (((mate, other)[lo], T - n), ((mate, other)[hi], 2 * T)):
                    value = buf[4 * side + tile, row:row + n]
                    ref[row_at(side, distance), to:to + n] = 1.0 - value if name == "flags" else value

    on_parity(place_corners)
    low, high = range(0, H), range(top - 1, top + H)
    for x in (*low, *high):
        a = sg[x]
        if x < top + H - 1:
            wx[x] = harmonic(a, sg[x + 1])
        if 0 < x < top + H - 1 and x != top - 1:
            wy[x] = harmonic(a, pltpu.roll(a, 3 * T - 1, 0))
            wz[x] = harmonic(a, jnp.where(last, a, pltpu.roll(a, nz - 1, 1)))

    def sweep(src, margin, store):
        for lo, hi in ((1 + margin, H + 1 + margin), (top - 1 - margin, top + 4 - margin)):
            below = wx[lo - 1] * (src[lo - 1] - src[lo])
            for x in range(lo, hi):
                value, below = laplace(src[x], src[x + 1], below, wx[x], wy[x], wz[x], sg[x], first, last)
                store(x, value)

    def store_v0(x, value):
        v0[x] = un[x] * (ch[x] - value)

    def apply_to(src, dst):
        def store(x, value):
            dst[x] = mapped(un[x], value, src[x])
        return store

    sweep(pv, 0, store_v0)
    sweep(v0, 1, apply_to(v0, v1))
    sweep(v1, 2, apply_to(v1, v2))
    acc = [sums[k] for k in range(6)]
    for lo, hi in ((H, H + 4), (top - 4, top)):
        below = wx[lo - 1] * (v2[lo - 1] - v2[lo])
        for x in range(lo, hi):
            value, below = laplace(v2[x], v2[x + 1], below, wx[x], wy[x], wz[x], sg[x], first, last)
            c = v2.own(x)
            d = mapped(un.own(x), value[T:2 * T], c)
            for k, term in enumerate(dots(v0.own(x), v1.own(x), c, d)):
                acc[k] = acc[k] + term
    rows = moments.shape[0]
    col = lax.broadcasted_iota(jnp.int32, (1, 128), 1)
    line = jnp.zeros((1, 128), F32)
    for k, value in enumerate(acc):
        total = jnp.sum(jnp.sum(value, axis=0, keepdims=True), axis=1, keepdims=True)
        line = jnp.where(col == k, total, line)
    moments[...] = jnp.broadcast_to(line, (rows, 128))


def cg_coefficients(mu):
    def form(p, shift):
        total = None
        for i, a in enumerate(p):
            for j, b in enumerate(p):
                term = a * b * mu[i + j + shift]
                total = term if total is None else total + term
        return total

    one = jnp.ones_like(mu[0])
    a0 = mu[0] / mu[1]
    r1 = (one, -a0)
    n1 = form(r1, 0)
    b0 = n1 / mu[0]
    p1 = (one + b0, -a0)
    a1 = n1 / form(p1, 1)
    r2 = (one, r1[1] - a1 * p1[0], -a1 * p1[1])
    n2 = form(r2, 0)
    b1 = n2 / n1
    p2 = (r2[0] + b1 * p1[0], r2[1] + b1 * p1[1], r2[2])
    a2 = n2 / form(p2, 1)
    return (a0 + a1 * p1[0] + a2 * p2[0], a1 * p1[1] + a2 * p2[1], a2 * p2[2])


def step_kernel(moments, base, gain, blocks, solids, pv, v0, v1, v2, pv_x, v0_x, v1_x, v2_x, xlo, xhi, rest_lo, rest_hi,
                potential_hbm, nxt_hbm, pot, nxt, potential, sem):
    nx, _, nz = solids.shape
    top = nx + H
    copies = [pltpu.make_async_copy(base.at[:, 0], nxt_hbm.at[:, 0], sem.at[1])]
    copies[0].start()
    row = jnp.sum(moments[...], axis=0, keepdims=True)
    col = lax.broadcasted_iota(jnp.int32, (1, 128), 1)
    mu = [jnp.sum(jnp.where(col == k, row, 0.0), axis=1, keepdims=True) for k in range(6)]
    coef = [c * SCALE for c in cg_coefficients(mu)]

    def correct(x):
        depth = min(x - H, top - 1 - x)
        out = x if x < 8 else x - (nx + 2 * H - 16)
        fields = ((v0, v0_x), (v1, v1_x), (v2, v2_x))
        terms = [
            c * (a[x] if depth > k else b[out]) for k, (c, (a, b)) in enumerate(zip(coef, fields))
        ]
        pot[x] = (pv[x] if depth >= 0 else pv_x[out]) + (terms[0] + terms[1] + terms[2])

    lane = lax.broadcasted_iota(jnp.int32, (T, nz), 1)
    line = lax.broadcasted_iota(jnp.int32, (T, nz), 0)

    def entering(species, way, current, dens, difference):
        sign = 1.0 if way % 2 == 1 else -1.0
        return at_rest(species, way, current, dens) + sign * response(species, dens) * difference

    def step(x):
        at = x + H
        mid = pot[at, T:2 * T]
        potential[x] = mid
        free = 1.0 - solids[x]
        dx = [pot[at + 1 + k, T:2 * T] - pot[at - 1 + k, T:2 * T] for k in (0, -1, 1)]
        near = {k: pot[at, T + k:2 * T + k] for k in (-2, -1, 1, 2)}
        dy = (near[1] - near[-1], mid - near[-2], near[2] - mid)
        dz = (jnp.where(lane == nz - 1, 0.0, pltpu.roll(mid, nz - 1, 1))
              - jnp.where(lane == 0, 0.0, pltpu.roll(mid, 1, 1)))
        dz = (dz, pltpu.roll(dz, 1, 1), pltpu.roll(dz, nz - 1, 1))
        difference = [None]
        for d in (dx, dy, dz):
            for k in (1, 2):
                block = blocks[len(difference) - 1, x]
                difference.append(jnp.where(block > 0.5, d[0], d[k]))
        for species in range(2):
            for i in range(1, 7):
                value = base[species, i, x] + gain[species, i - 1, x] * difference[i]
                if i in (3, 4):
                    rest, border, d = ((rest_lo, 0, dy[1]), (rest_hi, T - 1, dy[2]))[i - 3]

                    def face(first):
                        first -= 2 * T
                        return rest[x, first:first + 1]
                    here = slice(border, border + 1)
                    new = entering(species, i, face(POP + species), face(DENS + species), d[here])
                    new = jnp.where(face(SOLID) > 0.5, value[here], free[here] * new)
                    value = jnp.where(line == border, new, value)
                nxt[species, i - 1, x] = value

    def x_face(x, way, buf, d):
        free = 1.0 - solids[x]
        for species in range(2):
            new = entering(species, way, buf[POP + species], buf[DENS + species], d)
            nxt[species, way - 1, x] = jnp.where(buf[SOLID] > 0.5, nxt[species, way - 1, x], free * new)

    for x in range(H - 2, H + 2):
        correct(x)
    for first in range(0, nx, 2):
        for x in range(first, first + 2):
            correct(x + H + 2)
            step(x)
        if first == 0:
            x_face(0, 1, xlo, pot[H, T:2 * T] - pot[H - 2, T:2 * T])
        if first == nx - 2:
            x_face(nx - 1, 2, xhi, pot[top + 1, T:2 * T] - pot[top - 1, T:2 * T])
        rows = pl.ds(first, 2)
        copies.append(pltpu.make_async_copy(
            nxt.at[:, :, rows], nxt_hbm.at[:, 1:, rows], sem.at[2 + first // 2]))
        copies[-1].start()
    copies.append(pltpu.make_async_copy(potential, potential_hbm, sem.at[0]))
    copies[-1].start()
    for copy in copies:
        copy.wait()


def to_mate(block):
    n = lax.axis_size("gy")
    return lax.ppermute(block, "gy", [(i, i ^ 1) for i in range(n)])


def to_other(block):
    n = lax.axis_size("gy")
    return lax.ppermute(block, "gy", [(i, (i + (1 if i % 2 else -1)) % n) for i in range(n)])


def shift(block, axis, distance):
    n = lax.axis_size(axis)
    return lax.ppermute(block, axis, [(i, (i + distance) % n) for i in range(n)])


def local(populations, conductivity, deposit_mask, electrode_flags, previous_potential):
    nx, ny, nz = conductivity.shape
    brick = jax.ShapeDtypeStruct((nx, ny, nz), F32)
    x_face = jax.ShapeDtypeStruct((22, ny, nz), F32)
    y_face = jax.ShapeDtypeStruct((nx, FACE_ROWS, nz), F32)
    whole = jax.ShapeDtypeStruct(populations.shape, F32)
    arguments = (
        pltpu.with_memory_space_constraint(a, pltpu.HBM)
        for a in (populations, conductivity, deposit_mask, electrode_flags, previous_potential)
    )
    pops, sigma, solid, flags, prev, charge, xlo_s, xhi_s, y_mate, y_other = pl.pallas_call(
        load_kernel,
        out_shape=(whole, brick, brick, brick, brick, brick, x_face, x_face, y_face, y_face),
        in_specs=[HBM] * 5,
        out_specs=(VMEM,) * 10,
        scratch_shapes=[
            pltpu.VMEM((nx, ny, nz), F32),
            pltpu.VMEM((nx, ny, nz), jnp.int32),
            pltpu.VMEM((nx, ny, nz), jnp.int32),
            pltpu.SemaphoreType.DMA((8,)),
        ],
        compiler_params=params(16),
        name="load",
    )(*arguments)
    xlo = shift(xhi_s, "gx", 1)
    xhi = shift(xlo_s, "gx", -1)
    y_mate = to_mate(y_mate)
    y_other = to_other(y_other)
    six = jax.ShapeDtypeStruct((2, 6, nx, ny, nz), F32)
    base, gain, blocks = pl.pallas_call(
        prepare_kernel,
        out_shape=(whole, six, jax.ShapeDtypeStruct((6, nx, ny, nz), F32)),
        in_specs=[VMEM] * 2,
        out_specs=(VMEM,) * 3,
        scratch_shapes=[pltpu.VMEM(whole.shape, F32), pltpu.VMEM((2, nx, ny, nz), F32)],
        compiler_params=params(24),
        name="prepare",
    )(pops, solid)
    shape = (nx + 2 * H, 3 * T, nz)
    padded = jax.ShapeDtypeStruct(shape, F32)
    *fields, rest_lo, rest_hi = pl.pallas_call(
        start_kernel,
        out_shape=(padded,) * 8 + (brick, brick),
        in_specs=[VMEM] * 6,
        out_specs=(VMEM,) * 10,
        compiler_params=params(24),
        cost_estimate=pl.CostEstimate(flops=60_000_000, bytes_accessed=20_000_000, transcendentals=0),
        name="start",
    )(sigma, charge, flags, prev, y_mate, y_other)
    pv, sg, un, wx, wy, wz, v0, _ = fields
    corner = jax.ShapeDtypeStruct((8, ny, nz), F32)
    c_mate, c_other = pl.pallas_call(
        corner_kernel,
        out_shape=(corner, corner),
        in_specs=[VMEM] * 2 + [pl.BlockSpec(memory_space=pl.ANY)],
        out_specs=(VMEM,) * 2,
        compiler_params=params(8),
        name="corners",
    )(xlo, xhi, blocks)
    c_mate = to_mate(c_mate)
    c_other = to_other(c_other)
    v1, v2, sums = pl.pallas_call(
        inner_kernel,
        out_shape=(padded, padded, jax.ShapeDtypeStruct((6, ny, nz), F32)),
        in_specs=[VMEM] * 6,
        out_specs=(VMEM,) * 3,
        compiler_params=params(24),
        cost_estimate=pl.CostEstimate(flops=60_000_000, bytes_accessed=20_000_000, transcendentals=0),
        name="inner",
    )(sg, un, wx, wy, wz, v0)
    outer_shape = (16, 3 * T, nz)
    edges = jax.ShapeDtypeStruct(outer_shape, F32)
    count = lax.axis_size("gx") * lax.axis_size("gy")
    pv_x, v0_x, v1_x, v2_x, moments = pl.pallas_call(
        outer_kernel,
        out_shape=(edges,) * 4 + (jax.ShapeDtypeStruct((count, 128), F32),),
        in_specs=[VMEM] * 15,
        out_specs=(VMEM,) * 5,
        scratch_shapes=[pltpu.VMEM(outer_shape, F32)] * 6,
        compiler_params=params(28),
        name="outer",
    )(*fields, v1, v2, sums, xlo, xhi, c_mate, c_other)
    moments = lax.all_to_all(moments, ("gx", "gy"), 0, 0, tiled=True)
    return pl.pallas_call(
        step_kernel,
        out_shape=(brick, whole),
        in_specs=[VMEM] * 17,
        out_specs=(HBM,) * 2,
        scratch_shapes=[
            pltpu.VMEM(shape, F32),
            pltpu.VMEM(six.shape, F32),
            pltpu.VMEM((nx, ny, nz), F32),
            pltpu.SemaphoreType.DMA((2 + nx // 2,)),
        ],
        compiler_params=params(28),
        name="step",
    )(moments, base, gain, blocks, solid, pv, v0, v1, v2, pv_x, v0_x, v1_x, v2_x, xlo, xhi, rest_lo, rest_hi)


def solution(mesh):
    in_specs = (
        P(None, None, "gx", "gy", None),
        P("gx", "gy", None),
        P("gx", "gy", None),
        P("gx", "gy", None),
        P("gx", "gy", None),
    )
    out_specs = (P("gx", "gy", None), P(None, None, "gx", "gy", None))
    return jax.shard_map(local, mesh=mesh, in_specs=in_specs, out_specs=out_specs, check_vma=False)
```

```python
import jax
import jax.numpy as jnp
from jax import lax
from jax.experimental import pallas as pl
from jax.experimental.pallas import tpu as pltpu
from jax.sharding import PartitionSpec as P

SCREEN_RATE = 0.01
WEIGHTS = (0.25, 0.125, 0.125, 0.125, 0.125, 0.125, 0.125)
OPPOSITE = (0, 2, 1, 4, 3, 6, 5)
DRIFT_COEF = (-0.02, 0.016)
RELAX_TIME = (0.8, 1.1)

H = 5
T = 8
SCALE = 0.0625

PREV, SIGMA, FLAGS, CHARGE = (0, 5), (5, 5), (10, 4), (14, 3)
DENS, POP, SOLID = 17, 19, 21
Y_CHARGE = (14, 4)
Y_ROWS = 18
EXTRAS = 5

CORNER = (
    ("prev", 1, 4, 0, 0), ("prev", 2, 3, 0, 4), ("prev", 4, 1, 0, 7),
    ("sigma", 1, 4, 1, 0), ("sigma", 2, 3, 1, 4), ("sigma", 4, 1, 1, 7),
    ("prev", 3, 2, 2, 0), ("sigma", 3, 2, 2, 2), ("flags", 2, 2, 2, 4), ("charge", 2, 2, 2, 6),
    ("flags", 1, 3, 3, 0), ("charge", 1, 3, 3, 3), ("flags", 3, 1, 3, 6), ("charge", 3, 1, 3, 7),
)
SPAN = {"prev": PREV, "sigma": SIGMA, "flags": FLAGS, "charge": CHARGE}
VMEM = pl.BlockSpec(memory_space=pltpu.VMEM)
HBM = pl.BlockSpec(memory_space=pltpu.HBM)
F32 = jnp.float32


def params(mib):
    return pltpu.CompilerParams(vmem_limit_bytes=mib * 1024 * 1024)


def density(pops, species, x):
    d = pops[species, 0, x]
    for i in range(1, 7):
        d = d + pops[species, i, x]
    return d


def on_parity(run):
    odd = lax.rem(lax.axis_index("gy"), 2)
    pl.when(odd == 0)(lambda: run(0, 1))
    pl.when(odd == 1)(lambda: run(1, 0))


def load_kernel(pops_hbm, cond_hbm, mask_hbm, flags_hbm, prev_hbm,
                pops, sigma, solid, flags, prev, charge, xlo, xhi, other, mate, extra_other, extra_mate, cond, mask, marks, sem):
    nx = sigma.shape[0]
    quarter = nx // 4
    small = [
        pltpu.make_async_copy(src, dst, sem.at[4 + i])
        for i, (src, dst) in enumerate(
            ((cond_hbm, cond), (mask_hbm, mask), (flags_hbm, marks), (prev_hbm, prev))
        )
    ]
    large = [
        pltpu.make_async_copy(
            pops_hbm.at[:, :, pl.ds(q * quarter, quarter)],
            pops.at[:, :, pl.ds(q * quarter, quarter)],
            sem.at[q],
        )
        for q in range(4)
    ]
    for copy in small + large:
        copy.start()
    for copy in small:
        copy.wait()
    for x in range(nx):
        s = mask[x].astype(F32)
        solid[x] = s
        sigma[x] = cond[x] * (1.0 + 3.0 * s)
        flags[x] = marks[x].astype(F32)
    for out, up in ((xlo, False), (xhi, True)):
        for src, (first, n) in ((prev, PREV), (sigma, SIGMA), (flags, FLAGS)):
            at = nx - n if up else 0
            out[first:first + n] = src[at:at + n]
    for q in range(4):
        large[q].wait()
        rows = range(q * quarter, (q + 1) * quarter)
        on_parity(lambda lo, hi: pack_faces(
            pops, sigma, solid, flags, prev, charge, (other, mate)[lo], (other, mate)[hi],
            (extra_other, extra_mate)[lo], (extra_other, extra_mate)[hi], rows))
        if q in (0, 3):
            out, up, way = (xlo, False, 2) if q == 0 else (xhi, True, 1)
            first, n = CHARGE
            at = nx - n - 1 if up else 1
            out[first:first + n] = charge[at:at + n]
            edge = nx - 1 if up else 0
            for species in range(2):
                out[DENS + species] = density(pops, species, edge)
                out[POP + species] = pops[species, way, edge]
            out[SOLID] = solid[edge]


def pack_faces(pops, sigma, solid, flags, prev, charge, ylo, yhi, extra_lo, extra_hi, rows):
    for x in rows:
        d = (density(pops, 0, x), density(pops, 1, x))
        ch = 2.0 * d[0] - 2.0 * d[1]
        charge[x] = ch
        values = (prev[x], sigma[x], flags[x], ch)
        for out, extra, up, way in ((ylo, extra_lo, False, 4), (yhi, extra_hi, True, 3)):
            for value, (first, n) in zip(values, (PREV, SIGMA, FLAGS, Y_CHARGE)):
                at = T - n if up else 0
                out[x * Y_ROWS + first:x * Y_ROWS + first + n] = value[at:at + n]
            at = T - 1 if up else 0
            last = (*d, pops[0, way, x], pops[1, way, x], solid[x])
            for k, value in enumerate(last):
                extra[k, x:x + 1] = value[at:at + 1]


def at_rest(species, way, current, dens):
    return current - (1.0 / RELAX_TIME[species]) * (current - WEIGHTS[way] * dens)


def response(species, dens):
    return (0.5 * 4.0 * WEIGHTS[1] * DRIFT_COEF[species] / RELAX_TIME[species]) * dens


def prepare_kernel(pops, solids, base, gain, blocks, rest, resp):
    nx, _, nz = solids.shape
    lane = lax.broadcasted_iota(jnp.int32, (T, nz), 1)
    line = lax.broadcasted_iota(jnp.int32, (T, nz), 0)
    for x in range(nx):
        for species in range(2):
            dens = density(pops, species, x)
            resp[species, x] = response(species, dens)
            for i in range(7):
                rest[species, i, x] = at_rest(species, i, pops[species, i, x], dens)
    shifts = (None, None, None, (1, 0, line == 0), (T - 1, 0, line == T - 1),
              (1, 1, lane == 0), (nz - 1, 1, lane == nz - 1))
    for x in range(nx):
        solid = solids[x]
        free = 1.0 - solid
        for i in range(1, 7):
            sign = 1.0 if i % 2 == 1 else -1.0
            opposite = OPPOSITE[i]
            if i < 3:
                source = x - 1 if i == 1 else x + 1
                inside = 0 <= source < nx
                block = solids[source] if inside else jnp.ones_like(solid)

                def moved(value, index):
                    return value[(*index, source)]
            else:
                by, axis, border = shifts[i]
                inside = True
                block = jnp.where(border, 1.0, pltpu.roll(solid, by, axis))

                def moved(value, index):
                    return pltpu.roll(value[(*index, x)], by, axis)
            blocks[i - 1, x] = block
            for species in range(2):
                own, back = rest[species, opposite, x], resp[species, x]
                if inside:
                    own = jnp.where(block > 0.5, own, moved(rest, (species, i)))
                    back = jnp.where(block > 0.5, -back, moved(resp, (species,)))
                else:
                    back = -back
                base[species, i, x] = free * own
                gain[species, i - 1, x] = (sign * free) * back
        for species in range(2):
            base[species, 0, x] = free * rest[species, 0, x]


def x_row(buf, side, name, distance):
    if name == "charge":
        if distance == 1:
            return 2.0 * buf[DENS] - 2.0 * buf[DENS + 1]
        return buf[CHARGE[0] + (4 - distance if side == 0 else distance - 2)]
    first, n = SPAN[name]
    return buf[first + (n - distance if side == 0 else distance - 1)]


def corner_kernel(xlo, xhi, extra_other, extra_mate, blocks, other, mate, other_out, mate_out):
    other_out[...] = extra_other[...]
    mate_out[...] = extra_mate[...]
    on_parity(lambda lo, hi: pack_corners(xlo, xhi, (other, mate)[lo], (other, mate)[hi]))


def pack_corners(xlo, xhi, clo, chi):
    for side, buf in ((0, xlo), (1, xhi)):
        for name, distance, n, tile, at in CORNER:
            value = x_row(buf, side, name, distance)
            clo[4 * side + tile, at:at + n] = value[:n]
            chi[4 * side + tile, at:at + n] = value[T - n:]


def harmonic(a, b):
    return 2.0 * a * b / (a + b)


def laplace(m, above, below_flux, wx, wy, wz, sg, first, last):
    nz = m.shape[1]
    fx = wx * (m - above)
    fy = wy * (m - pltpu.roll(m, 3 * T - 1, 0))
    fz = wz * (m - jnp.where(last, 0.0, pltpu.roll(m, nz - 1, 1)))
    s = fx - below_flux
    s = s + (fy - pltpu.roll(fy, 1, 0))
    s = s + (fz + jnp.where(first, sg * m, -pltpu.roll(fz, 1, 1)))
    return s + SCREEN_RATE * m, fx


def mapped(u, value, v):
    return (u * value + (1.0 - u) * v) * SCALE


def ends(nz):
    lane = lax.broadcasted_iota(jnp.int32, (3 * T, nz), 1)
    return lane == 0, lane == nz - 1


def dots(a, b, c, d):
    return (a * a, a * b, b * b, b * c, c * c, c * d)


def place_faces(sigma, charge, flags, prev, ylo, yhi, pv, sg, un, ch):
    for x in range(sigma.shape[0]):
        at = x + H
        pv[at, T:2 * T] = prev[x]
        sg[at, T:2 * T] = sigma[x]
        un[at, T:2 * T] = 1.0 - flags[x]
        ch[at, T:2 * T] = charge[x]
        for buf, up in ((ylo, False), (yhi, True)):
            for ref, (first, n) in ((pv, PREV), (sg, SIGMA), (un, FLAGS), (ch, Y_CHARGE)):
                to = 2 * T if up else T - n
                value = buf[x * Y_ROWS + first:x * Y_ROWS + first + n]
                ref[at, to:to + n] = 1.0 - value if ref is un else value


def start_kernel(sigma, charge, flags, prev, other, mate,
                 pv, sg, un, wx, wy, wz, v0, ch):
    nx, _, nz = sigma.shape
    top = nx + H
    first, last = ends(nz)
    on_parity(lambda lo, hi: place_faces(
        sigma, charge, flags, prev, (other, mate)[lo], (other, mate)[hi], pv, sg, un, ch))

    def faces(x, a):
        b = sg[jnp.minimum(x + 1, top - 1)]
        wx[x] = harmonic(a, b)
        wy[x] = harmonic(a, pltpu.roll(a, 3 * T - 1, 0))
        wz[x] = harmonic(a, jnp.where(last, a, pltpu.roll(a, nz - 1, 1)))
        return b

    lax.fori_loop(H, top, faces, sg[H], unroll=4)

    def store_v0(x, value):
        v0[x] = un[x] * (ch[x] - value)

    inner_sweep(pv, H + 1, top - 1, store_v0, 7, wx, wy, wz, sg)


def inner_sweep(src, lo, hi, store, unroll, wx, wy, wz, sg):
    first, last = ends(src.shape[2])

    def body(x, below):
        value, below = laplace(src[x], src[x + 1], below, wx[x], wy[x], wz[x], sg[x], first, last)
        store(x, value)
        return below

    lax.fori_loop(lo, hi, body, wx[lo - 1] * (src[lo - 1] - src[lo]), unroll=unroll)


def inner_kernel(sg, un, wx, wy, wz, v0, v1, v2, sums):
    nx, nz = sg.shape[0] - 2 * H, sg.shape[2]
    top = nx + H
    first, last = ends(nz)

    def apply_to(src, dst):
        def store(x, value):
            dst[x] = mapped(un[x], value, src[x])
        return store

    inner_sweep(v0, H + 2, top - 2, apply_to(v0, v1), 6, wx, wy, wz, sg)
    inner_sweep(v1, H + 3, top - 3, apply_to(v1, v2), 5, wx, wy, wz, sg)

    def last_sweep(x, carry):
        below, acc = carry
        value, below = laplace(v2[x], v2[x + 1], below, wx[x], wy[x], wz[x], sg[x], first, last)
        a, b, c = v0[x, T:2 * T], v1[x, T:2 * T], v2[x, T:2 * T]
        d = mapped(un[x, T:2 * T], value[T:2 * T], c)
        return below, tuple(s + t for s, t in zip(acc, dots(a, b, c, d)))

    zero = jnp.zeros((T, nz), F32)
    below = wx[H + 3] * (v2[H + 3] - v2[H + 4])
    _, acc = lax.fori_loop(H + 4, top - 4, last_sweep, (below, (zero,) * 6), unroll=4)
    for k, value in enumerate(acc):
        sums[k] = value


def outer_kernel(pv_in, sg_in, un_in, wx_in, wy_in, wz_in, v0_in, ch_in, v1_in, v2_in, sums,
                 xlo, xhi, other, mate,
                 pv_out, v0_out, v1_out, v2_out, moments, sg_out, un_out, ch_out, wx_out, wy_out, wz_out):
    nx, nz = pv_in.shape[0] - 2 * H, pv_in.shape[2]
    top = nx + H
    first, last = ends(nz)

    def outer(x):
        return x if x < 8 else x - (nx + 2 * H - 16)

    class Rows:
        def __init__(self, inner, out, lo, hi):
            self.inner, self.out, self.lo, self.hi = inner, out, lo, hi

        def __getitem__(self, x):
            return self.inner[x] if self.lo <= x < self.hi else self.out[outer(x)]

        def own(self, x):
            if self.lo <= x < self.hi:
                return self.inner[x, T:2 * T]
            return self.out[outer(x), T:2 * T]

        def __setitem__(self, x, value):
            self.out[outer(x)] = value

    pv, sg, un = Rows(pv_in, pv_out, H, top), Rows(sg_in, sg_out, H, top), Rows(un_in, un_out, H, top)
    wx, wy, wz = Rows(wx_in, wx_out, H, top - 1), Rows(wy_in, wy_out, H, top), Rows(wz_in, wz_out, H, top)
    v0, v1, v2 = Rows(v0_in, v0_out, H + 1, top - 1), Rows(v1_in, v1_out, H + 2, top - 2), Rows(v2_in, v2_out, H + 3, top - 3)

    ch = Rows(ch_in, ch_out, H, top)

    def row_at(side, distance):
        return outer(H - distance if side == 0 else top - 1 + distance)

    for side, buf in ((0, xlo), (1, xhi)):
        for distance in range(1, 6):
            at = row_at(side, distance)
            pv_out[at, T:2 * T] = x_row(buf, side, "prev", distance)
            sg_out[at, T:2 * T] = x_row(buf, side, "sigma", distance)
            if distance < 5:
                un_out[at, T:2 * T] = 1.0 - x_row(buf, side, "flags", distance)
                ch_out[at, T:2 * T] = x_row(buf, side, "charge", distance)

    def place_corners(lo, hi):
        for side in range(2):
            for name, distance, n, tile, row in CORNER:
                ref = {"prev": pv_out, "sigma": sg_out, "flags": un_out, "charge": ch_out}[name]
                for buf, to in (((other, mate)[lo], T - n), ((other, mate)[hi], 2 * T)):
                    value = buf[4 * side + tile, row:row + n]
                    ref[row_at(side, distance), to:to + n] = 1.0 - value if name == "flags" else value

    on_parity(place_corners)
    low, high = range(0, H), range(top - 1, top + H)
    for x in (*low, *high):
        a = sg[x]
        if x < top + H - 1:
            wx[x] = harmonic(a, sg[x + 1])
        if 0 < x < top + H - 1 and x != top - 1:
            wy[x] = harmonic(a, pltpu.roll(a, 3 * T - 1, 0))
            wz[x] = harmonic(a, jnp.where(last, a, pltpu.roll(a, nz - 1, 1)))

    def sweep(src, margin, store):
        for lo, hi in ((1 + margin, H + 1 + margin), (top - 1 - margin, top + 4 - margin)):
            below = wx[lo - 1] * (src[lo - 1] - src[lo])
            for x in range(lo, hi):
                value, below = laplace(src[x], src[x + 1], below, wx[x], wy[x], wz[x], sg[x], first, last)
                store(x, value)

    def store_v0(x, value):
        v0[x] = un[x] * (ch[x] - value)

    def apply_to(src, dst):
        def store(x, value):
            dst[x] = mapped(un[x], value, src[x])
        return store

    sweep(pv, 0, store_v0)
    sweep(v0, 1, apply_to(v0, v1))
    sweep(v1, 2, apply_to(v1, v2))
    acc = [sums[k] for k in range(6)]
    for lo, hi in ((H, H + 4), (top - 4, top)):
        below = wx[lo - 1] * (v2[lo - 1] - v2[lo])
        for x in range(lo, hi):
            value, below = laplace(v2[x], v2[x + 1], below, wx[x], wy[x], wz[x], sg[x], first, last)
            c = v2.own(x)
            d = mapped(un.own(x), value[T:2 * T], c)
            for k, term in enumerate(dots(v0.own(x), v1.own(x), c, d)):
                acc[k] = acc[k] + term
    rows = moments.shape[0]
    col = lax.broadcasted_iota(jnp.int32, (1, 128), 1)
    line = jnp.zeros((1, 128), F32)
    for k, value in enumerate(acc):
        total = jnp.sum(jnp.sum(value, axis=0, keepdims=True), axis=1, keepdims=True)
        line = jnp.where(col == k, total, line)
    moments[...] = jnp.broadcast_to(line, (rows, 128))


def cg_coefficients(mu):
    def form(p, shift):
        total = None
        for i, a in enumerate(p):
            for j, b in enumerate(p):
                term = a * b * mu[i + j + shift]
                total = term if total is None else total + term
        return total

    one = jnp.ones_like(mu[0])
    a0 = mu[0] / mu[1]
    r1 = (one, -a0)
    n1 = form(r1, 0)
    b0 = n1 / mu[0]
    p1 = (one + b0, -a0)
    a1 = n1 / form(p1, 1)
    r2 = (one, r1[1] - a1 * p1[0], -a1 * p1[1])
    n2 = form(r2, 0)
    b1 = n2 / n1
    p2 = (r2[0] + b1 * p1[0], r2[1] + b1 * p1[1], r2[2])
    a2 = n2 / form(p2, 1)
    return (a0 + a1 * p1[0] + a2 * p2[0], a1 * p1[1] + a2 * p2[1], a2 * p2[2])


def step_kernel(moments, base, gain, blocks, solids, pv, v0, v1, v2, pv_x, v0_x, v1_x, v2_x, xlo, xhi, extra_other, extra_mate,
                potential_hbm, nxt_hbm, pot, nxt, potential, rest_lo, rest_hi, sem):
    nx, _, nz = solids.shape
    top = nx + H
    copies = [pltpu.make_async_copy(base.at[:, 0], nxt_hbm.at[:, 0], sem.at[1])]
    copies[0].start()

    def place_extras(lo, hi):
        rest_lo[...] = (extra_other, extra_mate)[lo][...]
        rest_hi[...] = (extra_other, extra_mate)[hi][...]

    on_parity(place_extras)
    row = jnp.sum(moments[...], axis=0, keepdims=True)
    col = lax.broadcasted_iota(jnp.int32, (1, 128), 1)
    mu = [jnp.sum(jnp.where(col == k, row, 0.0), axis=1, keepdims=True) for k in range(6)]
    coef = [c * SCALE for c in cg_coefficients(mu)]

    def correct(x):
        depth = min(x - H, top - 1 - x)
        out = x if x < 8 else x - (nx + 2 * H - 16)
        fields = ((v0, v0_x), (v1, v1_x), (v2, v2_x))
        terms = [
            c * (a[x] if depth > k else b[out]) for k, (c, (a, b)) in enumerate(zip(coef, fields))
        ]
        pot[x] = (pv[x] if depth >= 0 else pv_x[out]) + (terms[0] + terms[1] + terms[2])

    lane = lax.broadcasted_iota(jnp.int32, (T, nz), 1)
    line = lax.broadcasted_iota(jnp.int32, (T, nz), 0)

    def entering(species, way, current, dens, difference):
        sign = 1.0 if way % 2 == 1 else -1.0
        return at_rest(species, way, current, dens) + sign * response(species, dens) * difference

    def step(x):
        at = x + H
        mid = pot[at, T:2 * T]
        potential[x] = mid
        free = 1.0 - solids[x]
        dx = [pot[at + 1 + k, T:2 * T] - pot[at - 1 + k, T:2 * T] for k in (0, -1, 1)]
        near = {k: pot[at, T + k:2 * T + k] for k in (-2, -1, 1, 2)}
        dy = (near[1] - near[-1], mid - near[-2], near[2] - mid)
        dz = (jnp.where(lane == nz - 1, 0.0, pltpu.roll(mid, nz - 1, 1))
              - jnp.where(lane == 0, 0.0, pltpu.roll(mid, 1, 1)))
        dz = (dz, pltpu.roll(dz, 1, 1), pltpu.roll(dz, nz - 1, 1))
        difference = [None]
        for d in (dx, dy, dz):
            for k in (1, 2):
                block = blocks[len(difference) - 1, x]
                difference.append(jnp.where(block > 0.5, d[0], d[k]))
        for species in range(2):
            for i in range(1, 7):
                value = base[species, i, x] + gain[species, i - 1, x] * difference[i]
                if i in (3, 4):
                    rest, border, d = ((rest_lo, 0, dy[1]), (rest_hi, T - 1, dy[2]))[i - 3]

                    def face(first):
                        return rest[first - DENS, x:x + 1]
                    here = slice(border, border + 1)
                    new = entering(species, i, face(POP + species), face(DENS + species), d[here])
                    new = jnp.where(face(SOLID) > 0.5, value[here], free[here] * new)
                    value = jnp.where(line == border, new, value)
                nxt[species, i - 1, x] = value

    def x_face(x, way, buf, d):
        free = 1.0 - solids[x]
        for species in range(2):
            new = entering(species, way, buf[POP + species], buf[DENS + species], d)
            nxt[species, way - 1, x] = jnp.where(buf[SOLID] > 0.5, nxt[species, way - 1, x], free * new)

    for x in range(H - 2, H + 2):
        correct(x)
    for first in range(0, nx, 2):
        for x in range(first, first + 2):
            correct(x + H + 2)
            step(x)
        if first == 0:
            x_face(0, 1, xlo, pot[H, T:2 * T] - pot[H - 2, T:2 * T])
        if first == nx - 2:
            x_face(nx - 1, 2, xhi, pot[top + 1, T:2 * T] - pot[top - 1, T:2 * T])
        rows = pl.ds(first, 2)
        copies.append(pltpu.make_async_copy(
            nxt.at[:, :, rows], nxt_hbm.at[:, 1:, rows], sem.at[2 + first // 2]))
        copies[-1].start()
    copies.append(pltpu.make_async_copy(potential, potential_hbm, sem.at[0]))
    copies[-1].start()
    for copy in copies:
        copy.wait()


def to_mate(block):
    n = lax.axis_size("gy")
    return lax.ppermute(block, "gy", [(i, i ^ 1) for i in range(n)])


def to_other(block):
    n = lax.axis_size("gy")
    return lax.ppermute(block, "gy", [(i, (i + (1 if i % 2 else -1)) % n) for i in range(n)])


def shift(block, axis, distance):
    n = lax.axis_size(axis)
    return lax.ppermute(block, axis, [(i, (i + distance) % n) for i in range(n)])


def local(populations, conductivity, deposit_mask, electrode_flags, previous_potential):
    nx, ny, nz = conductivity.shape
    brick = jax.ShapeDtypeStruct((nx, ny, nz), F32)
    x_face = jax.ShapeDtypeStruct((22, ny, nz), F32)
    y_face = jax.ShapeDtypeStruct((nx * Y_ROWS, nz), F32)
    extra = jax.ShapeDtypeStruct((EXTRAS, nx, nz), F32)
    whole = jax.ShapeDtypeStruct(populations.shape, F32)
    arguments = (
        pltpu.with_memory_space_constraint(a, pltpu.HBM)
        for a in (populations, conductivity, deposit_mask, electrode_flags, previous_potential)
    )
    pops, sigma, solid, flags, prev, charge, xlo_s, xhi_s, y_other, y_mate, e_other, e_mate = pl.pallas_call(
        load_kernel,
        out_shape=(whole, brick, brick, brick, brick, brick, x_face, x_face, y_face, y_face, extra, extra),
        in_specs=[HBM] * 5,
        out_specs=(VMEM,) * 12,
        scratch_shapes=[
            pltpu.VMEM((nx, ny, nz), F32),
            pltpu.VMEM((nx, ny, nz), jnp.int32),
            pltpu.VMEM((nx, ny, nz), jnp.int32),
            pltpu.SemaphoreType.DMA((8,)),
        ],
        compiler_params=params(16),
        name="load",
    )(*arguments)
    xlo = shift(xhi_s, "gx", 1)
    xhi = shift(xlo_s, "gx", -1)
    y_other = to_other(y_other)
    y_mate = to_mate(y_mate)
    six = jax.ShapeDtypeStruct((2, 6, nx, ny, nz), F32)
    base, gain, blocks = pl.pallas_call(
        prepare_kernel,
        out_shape=(whole, six, jax.ShapeDtypeStruct((6, nx, ny, nz), F32)),
        in_specs=[VMEM] * 2,
        out_specs=(VMEM,) * 3,
        scratch_shapes=[pltpu.VMEM(whole.shape, F32), pltpu.VMEM((2, nx, ny, nz), F32)],
        compiler_params=params(24),
        name="prepare",
    )(pops, solid)
    shape = (nx + 2 * H, 3 * T, nz)
    padded = jax.ShapeDtypeStruct(shape, F32)
    fields = pl.pallas_call(
        start_kernel,
        out_shape=(padded,) * 8,
        in_specs=[VMEM] * 6,
        out_specs=(VMEM,) * 8,
        compiler_params=params(24),
        cost_estimate=pl.CostEstimate(flops=60_000_000, bytes_accessed=20_000_000, transcendentals=0),
        name="start",
    )(sigma, charge, flags, prev, y_other, y_mate)
    pv, sg, un, wx, wy, wz, v0, _ = fields
    corner = jax.ShapeDtypeStruct((8, ny, nz), F32)
    c_other, c_mate, e_other, e_mate = pl.pallas_call(
        corner_kernel,
        out_shape=(corner, corner, extra, extra),
        in_specs=[VMEM] * 4 + [pl.BlockSpec(memory_space=pl.ANY)],
        out_specs=(VMEM,) * 4,
        cost_estimate=pl.CostEstimate(flops=20_000_000_000, bytes_accessed=300_000_000, transcendentals=0),
        compiler_params=params(8),
        name="corners",
    )(xlo, xhi, e_other, e_mate, blocks)
    c_other = to_other(c_other)
    c_mate = to_mate(c_mate)
    e_other = to_other(e_other)
    e_mate = to_mate(e_mate)
    v1, v2, sums = pl.pallas_call(
        inner_kernel,
        out_shape=(padded, padded, jax.ShapeDtypeStruct((6, ny, nz), F32)),
        in_specs=[VMEM] * 6,
        out_specs=(VMEM,) * 3,
        compiler_params=params(24),
        cost_estimate=pl.CostEstimate(flops=60_000_000, bytes_accessed=20_000_000, transcendentals=0),
        name="inner",
    )(sg, un, wx, wy, wz, v0)
    outer_shape = (16, 3 * T, nz)
    edges = jax.ShapeDtypeStruct(outer_shape, F32)
    count = lax.axis_size("gx") * lax.axis_size("gy")
    pv_x, v0_x, v1_x, v2_x, moments = pl.pallas_call(
        outer_kernel,
        out_shape=(edges,) * 4 + (jax.ShapeDtypeStruct((count, 128), F32),),
        in_specs=[VMEM] * 15,
        out_specs=(VMEM,) * 5,
        scratch_shapes=[pltpu.VMEM(outer_shape, F32)] * 6,
        compiler_params=params(28),
        cost_estimate=pl.CostEstimate(flops=20_000_000_000, bytes_accessed=300_000_000, transcendentals=0),
        name="outer",
    )(*fields, v1, v2, sums, xlo, xhi, c_other, c_mate)
    moments, e_other, e_mate = lax.optimization_barrier((moments, e_other, e_mate))
    moments = lax.all_to_all(moments, ("gx", "gy"), 0, 0, tiled=True)
    return pl.pallas_call(
        step_kernel,
        out_shape=(brick, whole),
        in_specs=[VMEM] * 17,
        out_specs=(HBM,) * 2,
        scratch_shapes=[
            pltpu.VMEM(shape, F32),
            pltpu.VMEM(six.shape, F32),
            pltpu.VMEM((nx, ny, nz), F32),
            pltpu.VMEM(extra.shape, F32),
            pltpu.VMEM(extra.shape, F32),
            pltpu.SemaphoreType.DMA((2 + nx // 2,)),
        ],
        compiler_params=params(28),
        name="step",
    )(moments, base, gain, blocks, solid, pv, v0, v1, v2, pv_x, v0_x, v1_x, v2_x, xlo, xhi, e_other, e_mate)


def solution(mesh):
    in_specs = (
        P(None, None, "gx", "gy", None),
        P("gx", "gy", None),
        P("gx", "gy", None),
        P("gx", "gy", None),
        P("gx", "gy", None),
    )
    out_specs = (P("gx", "gy", None), P(None, None, "gx", "gy", None))
    return jax.shard_map(local, mesh=mesh, in_specs=in_specs, out_specs=out_specs, check_vma=False)
```
